32 devices in a mesh: dp: 16 (over z, x, core), seq: 2 (over y).
Axes of the slice: x: 2, y: 2, z: 4, core: 2. Of those that a mesh axis runs over, the one named last changes fastest.
Arguments:
- queries: bfloat16 [4096, 3072], P(('dp', 'seq')), may hold values from -6 to 6
- key_states: bfloat16 [4096, 3072], P(('dp', 'seq')), may hold values from -6 to 6
- value_states: bfloat16 [4096, 3072], P(('dp', 'seq')), may hold values from -6 to 6
- grad_out: bfloat16 [4096, 2560], P(('dp', 'seq')), may hold values from -6 to 6
- out_weight: bfloat16 [3072, 2560], P('seq', 'dp'), may hold values from -0.109375 to 0.109375
- key_blocks: int32 [24, 4, 4], replicated, may hold values from 0 to 3, as said below
- key_count: int32 [24, 4], replicated, may hold values from 4 to 4
Outputs:
- grad_queries: bfloat16 [4096, 3072], P(('dp', 'seq'))
- grad_keys: bfloat16 [4096, 3072], P(('dp', 'seq'))
- grad_weight: float32 [3072, 2560], P('seq', 'dp')
The draws below stay inside these ranges and needn't reach their ends.
Inputs may be any that keep to these rules, and one draw needn't show every extreme that they name: The first key_count[h, b] entries of key_blocks[h, b] name distinct key blocks; later entries name the other blocks and are not used. Query blocks 0 and 3 attend all 4 blocks; every other query block attends at most 4 blocks, and some reach 4 for every head.
All inputs are finite; a program needn't handle non-finite values.
Results may differ from the reference program's by a relative error of at most 0.0079.
Values may be sent and summed in bfloat16 or wider, within the bound.
No kernel may reach another device: no remote copies, remote signals or barrier semaphores. Data moves between devices by JAX's collectives and lax.ppermute only.
A program may use at most 128 MiB of HBM per device.

```python
import jax
import jax.numpy as jnp
from jax import lax

HEADS = 24
HD = 128
CW = 2560
BLK = 64
RANDB = 3
LENGTH = 256
NB = 4
TOKENS = 4096


def base_draw(key, salt):
    shape = (TOKENS, HEADS, HD)
    return jax.random.truncated_normal(jax.random.fold_in(key, salt), -6.0, 6.0, shape, jnp.float32)


def draw_queries(key, part):
    values = base_draw(key, 1)
    return values.reshape(TOKENS, HEADS * HD).astype(jnp.bfloat16)


def draw_key_states(key, part):
    values = base_draw(key, 2)
    return values.reshape(TOKENS, HEADS * HD).astype(jnp.bfloat16)


def layout(key):
    block_total = NB
    column = jnp.arange(block_total)
    block_row = jnp.arange(block_total)
    global_row = (block_row == 0) | (block_row == block_total - 1)
    mandatory = (column[None, :] == 0) | (column[None, :] == block_total - 1)
    mandatory = mandatory | (jnp.abs(column[None, :] - block_row[:, None]) <= 1) | global_row[:, None]
    extra = jax.random.randint(jax.random.fold_in(key, 21), (HEADS, block_total), 1, RANDB + 1)
    extra = jnp.where((block_row == block_total // 2)[None, :], RANDB, extra)
    counted = jnp.sum(mandatory.astype(jnp.int32), axis=-1)
    count_out = jnp.minimum(counted[None, :] + extra, block_total)
    noise = jax.random.randint(jax.random.fold_in(key, 22), (HEADS, block_total, block_total), 0, 4096)
    priority = jnp.where(mandatory[None], 1 << 24, 0) + noise * block_total + column[None, None, :]
    order = lax.top_k(priority, block_total)[1]
    return (order.astype(jnp.int32), count_out.astype(jnp.int32))


def draw_key_blocks(key, part):
    return layout(key)[0]


def draw_key_count(key, part):
    return layout(key)[1]


def spiked(result, own_key, source, target, shards_of, factor):
    def block_of(dim):
        return (jnp.arange(result.shape[dim]) // (result.shape[dim] // shards_of)).reshape((-1,) + (1,) * (result.ndim - 1 - dim))

    first = jax.random.permutation(own_key, shards_of)[block_of(target)]
    far = (block_of(target) + shards_of // 2) % shards_of
    return jnp.where((block_of(source) == first) | (block_of(source) == far), factor * result, result)


def shard_levels(stream_key, dims, split, least, largest):
    def one(dim, parts):
        heights = jax.random.uniform(jax.random.fold_in(jax.random.fold_in(stream_key, 6), dim), (parts,), jnp.float32, least / len(split), largest / len(split))
        return jnp.repeat(jnp.exp(heights), dims[dim] // parts).reshape((-1,) + (1,) * (len(dims) - dim - 1))

    level = one(*split[0])
    for cut in split[1:]:
        level = level * one(*cut)
    return level


def normal_values(rng, shape, scale, most, pieces=(), kind=jnp.bfloat16):
    values = scale * jax.random.normal(rng, shape, jnp.float32)
    if pieces:
        values = values * shard_levels(rng, shape, pieces, -0.22, 0.18)
    return jnp.clip(values, -most, most).astype(kind)


def noise_with(stream_key, dims, scale, limit, split, heavy, kind=jnp.bfloat16):
    result = scale * jax.random.normal(stream_key, dims, jnp.float32)
    if split:
        result = result * shard_levels(stream_key, dims, split, -0.22, 0.18)
    return jnp.clip(spiked(result, jax.random.fold_in(stream_key, 3), *heavy), -limit, limit).astype(kind)


def setup_inputs(seed: int = 0) -> dict:
    key_list = jax.random.split(jax.random.key(seed), 8)
    queries = draw_queries(jax.random.fold_in(key_list[7], 71), 0)
    key_states = draw_key_states(jax.random.fold_in(key_list[7], 71), 0)
    value_states = normal_values(key_list[2], (TOKENS, HEADS * HD), 1.0, 6.0, ((0, 32),))
    grad_out = noise_with(key_list[3], (TOKENS, CW), 1.0, 6.0, ((0, 32),), (0, 1, 32, 2.75))
    out_weight = normal_values(key_list[4], (HEADS * HD, CW), (HEADS * HD) ** -0.5, 0.109375, ((0, 2), (1, 16)))
    key_blocks = draw_key_blocks(jax.random.fold_in(key_list[7], 71), 0)
    key_count = draw_key_count(jax.random.fold_in(key_list[7], 71), 0)
    return {"queries": queries, "key_states": key_states, "value_states": value_states, "grad_out": grad_out, "out_weight": out_weight, "key_blocks": key_blocks, "key_count": key_count}


def reference(queries, key_states, value_states, grad_out, out_weight, key_blocks, key_count):
    block_total = LENGTH // BLK
    live_slots = jnp.arange(block_total)[None, None, :] < key_count[:, :, None]
    hits = (key_blocks[:, :, :, None] == jnp.arange(block_total)[None, None, None, :]) & live_slots[:, :, :, None]
    allowed = jnp.any(hits, axis=2)
    token_mask = jnp.repeat(jnp.repeat(allowed, BLK, axis=1), BLK, axis=2)
    weight_heads = out_weight.astype(jnp.float32).reshape(HEADS, HD, CW)
    scale = HD ** -0.5
    seq_total = TOKENS // LENGTH

    def split_heads(array_in):
        return array_in.astype(jnp.float32).reshape(LENGTH, HEADS, HD).transpose(1, 0, 2)

    def merge_heads(array_in):
        return array_in.transpose(1, 0, 2).reshape(LENGTH, HEADS * HD)

    def one_sequence(running_sum, inputs):
        query_seq, key_seq, value_seq, grad_seq = inputs
        query_f = split_heads(query_seq)
        key_f = split_heads(key_seq)
        value_f = split_heads(value_seq)
        grad_f = grad_seq.astype(jnp.float32)
        scores = jnp.einsum("hid,hjd->hij", query_f, key_f) * scale
        scores = jnp.where(token_mask, scores, -jnp.inf)
        row_max = jnp.max(scores, axis=-1, keepdims=True)
        expo = jnp.exp(scores - row_max)
        probs = expo / jnp.sum(expo, axis=-1, keepdims=True)
        probs_b = lax.optimization_barrier(probs.astype(jnp.bfloat16)).astype(jnp.float32)
        head_outputs = jnp.einsum("hij,hjd->hid", probs_b, value_f).astype(jnp.bfloat16)
        grad_heads = jnp.einsum("lc,hdc->hld", grad_f, weight_heads).astype(jnp.bfloat16)
        grad_heads = lax.optimization_barrier(grad_heads).astype(jnp.float32)
        dprob = jnp.einsum("hid,hjd->hij", grad_heads, value_f)
        row_delta = jnp.sum(probs * dprob, axis=-1, keepdims=True)
        dscore = (probs * (dprob - row_delta) * scale).astype(jnp.bfloat16)
        dscore = lax.optimization_barrier(dscore).astype(jnp.float32)
        grad_q = jnp.einsum("hij,hjd->hid", dscore, key_f).astype(jnp.bfloat16)
        grad_k = jnp.einsum("hij,hid->hjd", dscore, query_f).astype(jnp.bfloat16)
        outs_f = lax.optimization_barrier(head_outputs).astype(jnp.float32)
        running_sum = running_sum + jnp.einsum("hld,lc->hdc", outs_f, grad_f).reshape(HEADS * HD, CW)
        return running_sum, (merge_heads(grad_q), merge_heads(grad_k))

    inputs = (queries.reshape(seq_total, LENGTH, HEADS * HD),
              key_states.reshape(seq_total, LENGTH, HEADS * HD),
              value_states.reshape(seq_total, LENGTH, HEADS * HD),
              grad_out.reshape(seq_total, LENGTH, CW))
    start_sum = jnp.zeros((HEADS * HD, CW), jnp.float32)
    grad_weight, (grad_queries, grad_keys) = lax.scan(one_sequence, start_sum, inputs)
    return grad_queries.reshape(TOKENS, HEADS * HD), grad_keys.reshape(TOKENS, HEADS * HD), grad_weight
```

```python
import functools

import jax
import jax.numpy as jnp
from jax import lax
from jax.experimental import pallas as pl
from jax.experimental.pallas import tpu as pltpu
from jax.sharding import PartitionSpec as P

HEADS = 24
HD = 128
BLK = 64
SCALE = HD ** (-0.5)
QUERY_TILE = 256
VMEM_LIMIT = 48 * 1024 * 1024
GROUP = 4


def dot(left, right, left_dim, right_dim):
    return lax.dot_general(
        left, right, (((left_dim,), (right_dim,)), ((), ())), preferred_element_type=jnp.float32
    )


def softmax_rows(query_rows, key_rows, bias_ref, head, first_block, block_count):
    scores = dot(query_rows, key_rows, 1, 1) * SCALE
    length = key_rows.shape[0]
    bias = jnp.concatenate(
        [
            jnp.broadcast_to(bias_ref[head, block : block + 1, :], (BLK, length))
            for block in range(first_block, first_block + block_count)
        ],
        axis=0,
    )
    scores = scores + bias
    row_max = jnp.max(scores, axis=-1, keepdims=True)
    expo = jnp.exp(scores - row_max)
    return expo * (1.0 / jnp.sum(expo, axis=-1, keepdims=True))


def take_tokens(own_ref, recv_refs, slot, columns):
    return jnp.concatenate(
        [own_ref[:, columns]] + [recv_ref[slot, :, columns] for recv_ref in recv_refs], axis=0
    )


def forward_kernel(heads_step, recv_count, pos_ref, *refs):
    query_ref, key_ref, value_ref = refs[:3]
    recv_refs = refs[3 : 3 + recv_count]
    bias_ref, out_ref = refs[3 + recv_count :]
    length = out_ref.shape[0]
    tile = min(QUERY_TILE, length)
    for head in range(heads_step):
        columns = slice(head * HD, (head + 1) * HD)
        query = take_tokens(query_ref, recv_refs, 0, columns)
        key = take_tokens(key_ref, recv_refs, 1, columns)
        value = take_tokens(value_ref, recv_refs, 2, columns)
        for start in range(0, length, tile):
            rows = slice(start, start + tile)
            probs = softmax_rows(query[rows], key, bias_ref, head, start // BLK, tile // BLK)
            out_ref[rows, columns] = dot(probs.astype(jnp.bfloat16), value, 1, 0).astype(
                jnp.bfloat16
            )


def backward_kernel(heads_step, recv_count, pos_ref, *refs):
    query_ref, key_ref, value_ref = refs[:3]
    recv_refs = refs[3 : 3 + recv_count]
    bias_ref, grad_ref, grad_recv_ref = refs[3 + recv_count : 6 + recv_count]
    out_refs = refs[6 + recv_count :]
    tokens = query_ref.shape[0]
    length = grad_ref.shape[0]
    tile = min(QUERY_TILE, length)
    for head in range(heads_step):
        columns = slice(head * HD, (head + 1) * HD)
        query = take_tokens(query_ref, recv_refs, 0, columns)
        key = take_tokens(key_ref, recv_refs, 1, columns)
        value = take_tokens(value_ref, recv_refs, 2, columns)
        grad_key = None
        for start in range(0, length, tile):
            rows = slice(start, start + tile)
            probs = softmax_rows(query[rows], key, bias_ref, head, start // BLK, tile // BLK)
            grad = grad_ref[rows, columns] + grad_recv_ref[rows, columns].astype(jnp.float32)
            dprob = dot(grad.astype(jnp.bfloat16), value, 1, 1)
            delta = jnp.sum(probs * dprob, axis=-1, keepdims=True)
            dscore = (probs * (dprob - delta) * SCALE).astype(jnp.bfloat16)
            grad_query = dot(dscore, key, 1, 0).astype(jnp.bfloat16)
            for piece in range(tile // tokens):
                out_refs[start // tokens + piece][0, :, columns] = grad_query[
                    piece * tokens : (piece + 1) * tokens
                ]
            part = dot(dscore, query[rows], 0, 0)
            grad_key = part if grad_key is None else grad_key + part
        grad_key = grad_key.astype(jnp.bfloat16)
        for piece in range(length // tokens):
            out_refs[piece][1, :, columns] = grad_key[piece * tokens : (piece + 1) * tokens]


def attention_specs(tokens, seq_size, local_heads, first, heads_step, bias):
    width = heads_step * HD
    own = pl.BlockSpec(
        (tokens, width), lambda h, pos: (0, (pos[0] * local_heads + first) // heads_step + h)
    )
    recv = pl.BlockSpec((3, tokens, width), lambda h, pos: (0, 0, h))
    bias_spec = pl.BlockSpec(
        (heads_step,) + bias.shape[1:], lambda h, pos: (first // heads_step + h, 0, 0)
    )
    return [own] * 3 + [recv] * (seq_size - 1) + [bias_spec]


def attention_cost(count, length, matmuls):
    return pl.CostEstimate(
        flops=count * matmuls * 2 * length * length * HD,
        bytes_accessed=count * length * HD * 2 * 5,
        transcendentals=count * length * length,
    )


def attend_forward(pos, own, recv, bias, first, count, local_heads, heads_step):
    tokens = own[0].shape[0]
    length = bias.shape[2]
    return pl.pallas_call(
        functools.partial(forward_kernel, heads_step, len(recv)),
        grid_spec=pltpu.PrefetchScalarGridSpec(
            num_scalar_prefetch=1,
            grid=(count // heads_step,),
            in_specs=attention_specs(
                tokens, len(recv) + 1, local_heads, first, heads_step, bias
            ),
            out_specs=pl.BlockSpec((length, heads_step * HD), lambda h, pos: (0, h)),
        ),
        out_shape=jax.ShapeDtypeStruct((length, count * HD), jnp.bfloat16),
        compiler_params=pltpu.CompilerParams(vmem_limit_bytes=VMEM_LIMIT),
        cost_estimate=attention_cost(count, length, 2),
        name="attend_forward",
    )(pos, *own, *recv, bias)


def attend_backward(pos, own, recv, bias, grad, grad_recv, first, count, local_heads, heads_step):
    tokens = own[0].shape[0]
    length = bias.shape[2]
    width = heads_step * HD
    grad_spec = pl.BlockSpec((length, width), lambda h, pos: (0, h))
    return pl.pallas_call(
        functools.partial(backward_kernel, heads_step, len(recv)),
        grid_spec=pltpu.PrefetchScalarGridSpec(
            num_scalar_prefetch=1,
            grid=(count // heads_step,),
            in_specs=attention_specs(tokens, len(recv) + 1, local_heads, first, heads_step, bias)
            + [grad_spec, grad_spec],
            out_specs=[
                pl.BlockSpec((2, tokens, width), lambda h, pos: (0, 0, h))
                for _ in range(len(recv) + 1)
            ],
        ),
        out_shape=[
            jax.ShapeDtypeStruct((2, tokens, count * HD), jnp.bfloat16)
            for _ in range(len(recv) + 1)
        ],
        compiler_params=pltpu.CompilerParams(vmem_limit_bytes=VMEM_LIMIT),
        cost_estimate=attention_cost(count, length, 5),
        name="attend_backward",
    )(pos, *own, *recv, bias, grad, grad_recv)


def bit_reversed(count):
    order = [0]
    while len(order) < count:
        order = [2 * value for value in order] + [2 * value + 1 for value in order]
    return order


def swap_with(array_in, axis_name, distance):
    size = lax.axis_size(axis_name)
    return lax.ppermute(array_in, axis_name, [(i, i ^ distance) for i in range(size)])


def mask_bias(lists_here, counts_here, place, seq_size, length):
    block_total = length // BLK
    per_part = block_total // seq_size
    lists_rel = jnp.concatenate(
        [
            lax.dynamic_slice_in_dim(lists_here, (place ^ k) * per_part, per_part, 1)
            for k in range(seq_size)
        ],
        axis=1,
    )
    counts_rel = jnp.concatenate(
        [
            lax.dynamic_slice_in_dim(counts_here, (place ^ k) * per_part, per_part, 1)
            for k in range(seq_size)
        ],
        axis=1,
    )
    token = jnp.arange(length)
    part_tokens = per_part * BLK
    token_block = (place ^ (token // part_tokens)) * per_part + (token % part_tokens) // BLK
    live = jnp.arange(block_total)[None, None, :] < counts_rel[:, :, None]
    hits = (lists_rel[:, :, :, None] == token_block) & live[:, :, :, None]
    return jnp.where(jnp.any(hits, axis=2), 0.0, -jnp.inf).astype(jnp.float32)


def per_device(queries, key_states, value_states, grad_out, out_weight, key_blocks, key_count):
    seq_size = lax.axis_size("seq")
    dp_size = lax.axis_size("dp")
    layers = dp_size // GROUP
    place = lax.axis_index("seq")
    row = lax.axis_index("dp")
    tokens = queries.shape[0]
    length = tokens * seq_size
    local_heads = HEADS // seq_size
    cols = out_weight.shape[1]
    own = (queries, key_states, value_states)
    pos = place.astype(jnp.int32).reshape(1)
    parts = 2 if local_heads % 2 == 0 else 1
    count = local_heads // parts
    heads_step = 2 if count % 2 == 0 else 1
    width = count * HD
    layer_order = bit_reversed(layers)

    def send_heads(part):
        received = []
        for k in range(1, seq_size):
            start = ((place ^ k) * local_heads + part * count) * HD
            sent = jnp.stack([lax.dynamic_slice_in_dim(a, start, width, 1) for a in own])
            received.append(swap_with(sent, "seq", k))
        return received

    def gather_rows(part):
        held = {0: out_weight[part * width : (part + 1) * width].T}
        bit = layers // 2
        while bit:
            for known in sorted(held):
                held[known ^ bit] = swap_with(held[known], "dp", bit * GROUP)
            bit //= 2
        return jnp.concatenate([held[k] for k in layer_order], axis=0)

    def gather_grad():
        turned = grad_out.T.reshape(dp_size, cols, tokens)
        order = jnp.array(
            [
                (layer << 2) | (dx << 1) | dc
                for dx in range(2)
                for dc in range(2)
                for layer in layer_order
            ],
            jnp.int32,
        )
        turned = jnp.take(turned, row ^ order, axis=0, mode="clip")
        turned = turned.reshape(2, 2, layers * cols, tokens)
        from_x = swap_with(turned[1], "dp", 2)
        from_c = swap_with(jnp.stack([turned[0, 1], from_x[1]]), "dp", 1)
        held = jnp.stack([turned[0, 0], from_x[0], from_c[0], from_c[1]])
        pieces = [held] + [swap_with(held, "seq", k) for k in range(1, seq_size)]
        return jnp.concatenate(pieces, axis=2)

    received = [send_heads(part) for part in range(parts)]
    rows_all = [gather_rows(part) for part in range(parts)]
    grad_cols = gather_grad()
    grad_wide = jnp.concatenate([grad_cols[i] for i in range(GROUP)], axis=1)

    first_head = place * local_heads
    bias = mask_bias(
        lax.dynamic_slice_in_dim(key_blocks, first_head, local_heads, 0),
        lax.dynamic_slice_in_dim(key_count, first_head, local_heads, 0),
        place,
        seq_size,
        length,
    )

    weight_parts = []
    own_parts = []
    back_parts = []
    for part in range(parts):
        first = part * count
        outs = attend_forward(
            pos, own, received[part], bias, first, count, local_heads, heads_step
        )
        outs_x = swap_with(outs, "dp", 2)
        outs_c = swap_with(outs, "dp", 1)
        outs_xc = swap_with(outs_x, "dp", 1)
        outs_wide = jnp.concatenate([outs, outs_x, outs_c, outs_xc], axis=0)
        block = grad_wide
        bit = 1
        half = block.shape[0] // 2
        sent = dot(block[half:], outs_wide, 1, 0).astype(jnp.bfloat16)
        kept = dot(block[:half], outs_wide, 1, 0)
        while True:
            kept = kept + swap_with(sent, "dp", bit * GROUP).astype(jnp.float32)
            bit *= 2
            if bit >= layers:
                break
            half = kept.shape[0] // 2
            sent = kept[half:].astype(jnp.bfloat16)
            kept = kept[:half]
        weight_parts.append(kept.T)

        def partial(sequence):
            return dot(grad_cols[sequence], rows_all[part], 0, 0)

        sent = jnp.stack([partial(2), partial(3)]).astype(jnp.bfloat16)
        got = swap_with(sent, "dp", 1).astype(jnp.float32)
        sent = (partial(1) + got[1]).astype(jnp.bfloat16)
        kept = partial(0) + got[0]
        got = swap_with(sent, "dp", 2)
        grads = attend_backward(
            pos, own, received[part], bias, kept, got, first, count, local_heads, heads_step
        )
        own_parts.append(grads[0])
        back_parts.append([swap_with(grads[k], "seq", k) for k in range(1, seq_size)])

    sections = [jnp.concatenate(own_parts, axis=2)] + [
        jnp.concatenate([back_parts[part][k] for part in range(parts)], axis=2)
        for k in range(seq_size - 1)
    ]
    if seq_size == 2:
        both = jnp.where(
            place == 0,
            jnp.concatenate(sections, axis=2),
            jnp.concatenate(sections[::-1], axis=2),
        )
    else:
        stacked = jnp.take(jnp.stack(sections), place ^ jnp.arange(seq_size), axis=0, mode="clip")
        both = stacked.transpose(1, 2, 0, 3).reshape(2, tokens, HEADS * HD)
    return (both[0], both[1], jnp.concatenate(weight_parts, axis=0))


def solution(mesh):
    return jax.shard_map(
        per_device,
        mesh=mesh,
        in_specs=(
            P(("dp", "seq"), None),
            P(("dp", "seq"), None),
            P(("dp", "seq"), None),
            P(("dp", "seq"), None),
            P("seq", "dp"),
            P(),
            P(),
        ),
        out_specs=(P(("dp", "seq"), None), P(("dp", "seq"), None), P("seq", "dp")),
        check_vma=False,
    )
```

```python
import functools
import math

import jax
import jax.numpy as jnp
from jax import lax
from jax.experimental import pallas as pl
from jax.experimental.pallas import tpu as pltpu
from jax.sharding import PartitionSpec as P

HEADS = 24
HD = 128
BLK = 64
SCALE = HD ** (-0.5)
QUERY_TILE = 256
VMEM_LIMIT = 16 * 1024 * 1024
COLLECT_VMEM = 63 * 1024 * 1024
GROUP = 4
SMALL_COST = pl.CostEstimate(flops=0, bytes_accessed=0, transcendentals=0)
PARTS = (6, 6)


def dot(left, right, left_dim, right_dim):
    return lax.dot_general(
        left, right, (((left_dim,), (right_dim,)), ((), ())), preferred_element_type=jnp.float32
    )


def whole(count, space=pltpu.VMEM):
    return [pl.BlockSpec(memory_space=space)] * count


def mask_rows(mask_ref, place, head, block_total, per_part):
    blocks = [
        (place ^ (block // per_part)) * per_part + block % per_part for block in range(block_total)
    ]
    bits = [mask_ref[head, block] for block in blocks]
    lane = lax.div(lax.broadcasted_iota(jnp.int32, (1, block_total * BLK), 1), jnp.int32(BLK))
    rows = []
    for block in blocks:
        row = jnp.zeros(lane.shape, jnp.float32)
        for query_block in range(block_total):
            allowed = lax.shift_right_logical(bits[query_block], block) & 1
            value = jnp.where(allowed == 1, 0.0, -jnp.inf).astype(jnp.float32)
            row = jnp.where(lane == query_block, value, row)
        rows.append(row)
    return rows


def softmax_columns(key_rows, query_rows, mask, queries):
    scores = dot(key_rows, query_rows, 1, 1) * SCALE
    bias = jnp.concatenate(
        [jnp.broadcast_to(row[:, queries], (BLK, scores.shape[1])) for row in mask], axis=0
    )
    scores = scores + bias
    column_max = jnp.max(scores, axis=0, keepdims=True)
    expo = jnp.exp(scores - column_max)
    return expo * (1.0 / jnp.sum(expo, axis=0, keepdims=True))


def each_head(count, body):
    step = 4 if count % 4 == 0 else 3 if count % 3 == 0 else 2 if count % 2 == 0 else 1

    def run(index, carry):
        for offset in range(step):
            body(index * step + offset)
        return carry

    lax.fori_loop(0, count // step, run, 0)


def head_tokens(piece_refs, columns):
    return [
        jnp.concatenate([piece_ref[slot, :, columns] for piece_ref in piece_refs], axis=0)
        for slot in range(3)
    ]


def lanes(head):
    return pl.ds(pl.multiple_of(head * HD, HD), HD)


def forward_kernel(first, count, local_heads, pos_ref, mask_ref, *refs):
    piece_refs, (out_ref, probs_ref) = refs[:-2], refs[-2:]
    length = out_ref.shape[1]
    tokens = length // len(piece_refs)
    tile = min(QUERY_TILE, length)
    place = pos_ref[0]

    def one(head):
        query, key, value = head_tokens(piece_refs, lanes(head))
        mask = mask_rows(
            mask_ref, place, place * local_heads + first + head, length // BLK, tokens // BLK
        )
        for start in range(0, length, tile):
            rows = slice(start, start + tile)
            probs = softmax_columns(key, query[rows], mask, rows)
            probs_ref[head, :, rows] = probs
            out_ref[lanes(head), rows] = dot(value, probs.astype(jnp.bfloat16), 0, 0).astype(
                jnp.bfloat16
            )

    each_head(count, one)


def backward_kernel(count, pieces, *refs):
    piece_refs, (probs_ref, grad_ref, grad_recv_ref) = refs[:pieces], refs[pieces : pieces + 3]
    out_refs = refs[pieces + 3 :]
    length = grad_ref.shape[0]
    tokens = length // pieces
    tile = min(QUERY_TILE, length)

    def one(head):
        columns = lanes(head)
        query, key, value = head_tokens(piece_refs, columns)
        grad_key = None
        for start in range(0, length, tile):
            rows = slice(start, start + tile)
            probs = probs_ref[head, :, rows]
            grad = grad_ref[rows, columns] + grad_recv_ref[rows, columns].astype(jnp.float32)
            dprob = dot(value, grad.astype(jnp.bfloat16), 1, 1)
            delta = jnp.sum(probs * dprob, axis=0, keepdims=True)
            dscore = (probs * (dprob - delta) * SCALE).astype(jnp.bfloat16)
            grad_query = dot(dscore, key, 0, 0).astype(jnp.bfloat16)
            for piece in range(tile // tokens):
                out_refs[start // tokens + piece][0, :, columns] = grad_query[
                    piece * tokens : (piece + 1) * tokens
                ]
            part = dot(dscore, query[rows], 1, 0)
            grad_key = part if grad_key is None else grad_key + part
        grad_key = grad_key.astype(jnp.bfloat16)
        for piece in range(length // tokens):
            out_refs[piece][1, :, columns] = grad_key[piece * tokens : (piece + 1) * tokens]

    each_head(count, one)


def attend_forward(pos, mask, pieces, first, count, local_heads):
    length = pieces[0].shape[1] * len(pieces)
    return pl.pallas_call(
        functools.partial(forward_kernel, first, count, local_heads),
        in_specs=whole(2, pltpu.SMEM) + whole(len(pieces)),
        out_specs=whole(2),
        out_shape=[
            jax.ShapeDtypeStruct((count * HD, length), jnp.bfloat16),
            jax.ShapeDtypeStruct((count, length, length), jnp.float32),
        ],
        compiler_params=pltpu.CompilerParams(vmem_limit_bytes=VMEM_LIMIT),
        cost_estimate=SMALL_COST,
        name="attend_forward",
    )(pos, mask, *pieces)


def attend_backward(pieces, probs, grad, grad_recv, count):
    tokens = pieces[0].shape[1]
    return pl.pallas_call(
        functools.partial(backward_kernel, count, len(pieces)),
        in_specs=whole(3 + len(pieces)),
        out_specs=whole(len(pieces)),
        out_shape=[jax.ShapeDtypeStruct((2, tokens, count * HD), jnp.bfloat16)] * len(pieces),
        compiler_params=pltpu.CompilerParams(vmem_limit_bytes=VMEM_LIMIT),
        cost_estimate=SMALL_COST,
        name="attend_backward",
    )(*pieces, probs, grad, grad_recv)


def collect_kernel(local_heads, pieces, pos_ref, *refs):
    sources, out_refs, sems = refs[:3], refs[3:-1], refs[-1]
    copies = []
    for out_ref, (distance, first, count) in zip(out_refs, pieces):
        start = pl.multiple_of(((pos_ref[0] ^ distance) * local_heads + first) * HD, HD)
        for slot, source in enumerate(sources):
            copies.append(
                pltpu.make_async_copy(
                    source.at[:, pl.ds(start, count * HD)],
                    out_ref.at[slot],
                    sems.at[len(copies)],
                )
            )
    for copy in copies:
        copy.start()
    for copy in copies:
        copy.wait()


def pick_kernel(local_heads, pieces, pos_ref, *refs):
    sources, out_refs = refs[:3], refs[3:]
    for out_ref, (distance, first, count) in zip(out_refs, pieces):
        start = pl.multiple_of(((pos_ref[0] ^ distance) * local_heads + first) * HD, HD)
        for slot, source in enumerate(sources):
            out_ref[slot] = source[:, pl.ds(start, count * HD)]


def pick_columns(pos, sources, local_heads, pieces):
    tokens = sources[0].shape[0]
    return pl.pallas_call(
        functools.partial(pick_kernel, local_heads, pieces),
        in_specs=whole(1, pltpu.SMEM) + whole(len(sources)),
        out_specs=whole(len(pieces)),
        out_shape=[
            jax.ShapeDtypeStruct((len(sources), tokens, count * HD), sources[0].dtype)
            for _, _, count in pieces
        ],
        compiler_params=pltpu.CompilerParams(vmem_limit_bytes=VMEM_LIMIT),
        cost_estimate=SMALL_COST,
        name="pick_columns",
    )(pos, *sources)


def collect_columns(pos, sources, local_heads, pieces):
    tokens = sources[0].shape[0]
    shapes = [(len(sources), tokens, count * HD) for _, _, count in pieces]
    return pl.pallas_call(
        functools.partial(collect_kernel, local_heads, pieces),
        in_specs=whole(1, pltpu.SMEM) + whole(len(sources), pltpu.HBM),
        out_specs=whole(len(pieces)),
        out_shape=[jax.ShapeDtypeStruct(shape, sources[0].dtype) for shape in shapes],
        scratch_shapes=[pltpu.SemaphoreType.DMA((len(sources) * len(pieces),))],
        compiler_params=pltpu.CompilerParams(vmem_limit_bytes=COLLECT_VMEM),
        cost_estimate=SMALL_COST,
        name="collect_columns",
    )(pos, *sources)


def turn_kernel(row_ref, grad_ref, near_ref, far_ref, held_ref):
    blocks, cols, _ = held_ref.shape
    layers = blocks // GROUP
    for block in range(blocks):
        held_ref[block] = grad_ref[:, block * cols : (block + 1) * cols].T
    for dc in range(2):
        for slot, layer in enumerate(bit_reversed(layers)):
            rows = slice(slot * cols, (slot + 1) * cols)
            near_ref[dc, rows] = held_ref[row_ref[0] ^ (GROUP * layer + dc)]
            far_ref[dc, rows] = held_ref[row_ref[0] ^ (GROUP * layer + 2 + dc)]


def turn_columns(row, grad, dp_size):
    tokens, cols = grad.shape[0], grad.shape[1] // dp_size
    layers = dp_size // GROUP
    if cols % 16:
        turned = grad.T.reshape(dp_size, cols, tokens)
        order = [GROUP * layer + kind for kind in range(GROUP) for layer in bit_reversed(layers)]
        turned = jnp.take(turned, row ^ jnp.array(order, jnp.int32), axis=0, mode="clip")
        turned = turned.reshape(2, 2, layers * cols, tokens)
        return turned[0], turned[1]
    return pl.pallas_call(
        turn_kernel,
        in_specs=whole(1, pltpu.SMEM) + whole(1),
        out_specs=whole(2),
        out_shape=[jax.ShapeDtypeStruct((2, layers * cols, tokens), grad.dtype)] * 2,
        scratch_shapes=[pltpu.VMEM((dp_size, cols, tokens), grad.dtype)],
        compiler_params=pltpu.CompilerParams(vmem_limit_bytes=VMEM_LIMIT),
        cost_estimate=SMALL_COST,
        name="turn_columns",
    )(row.astype(jnp.int32).reshape(1), grad)


def join_kernel(*refs):
    piece_refs, wide_ref, turned_ref = refs[:-2], refs[-2], refs[-1]
    tokens = piece_refs[0].shape[2]
    column = 0
    for sequence in range(2):
        for piece_ref in piece_refs:
            piece = piece_ref[sequence]
            wide_ref[:, column : column + tokens] = piece
            turned_ref[column : column + tokens, :] = piece.T
            column += tokens


def join_pieces(pieces):
    _, depth, tokens = pieces[0].shape
    width = 2 * tokens * len(pieces)
    return pl.pallas_call(
        join_kernel,
        in_specs=whole(len(pieces)),
        out_specs=whole(2),
        out_shape=[
            jax.ShapeDtypeStruct((depth, width), jnp.bfloat16),
            jax.ShapeDtypeStruct((width, depth), jnp.bfloat16),
        ],
        compiler_params=pltpu.CompilerParams(vmem_limit_bytes=VMEM_LIMIT),
        cost_estimate=SMALL_COST,
        name="join_pieces",
    )(*pieces)


def partial_kernel(first, count, grad_ref, grad_core_ref, *refs):
    weight_refs, (kept_ref, sent_ref) = refs[:-2], refs[-2:]
    length = kept_ref.shape[0]
    grad = jnp.concatenate([grad_ref[...], grad_core_ref[...]], axis=1)
    width = 2 * HD if count % 2 == 0 else HD
    for start in range(0, count * HD, width):
        rows = slice(first * HD + start, first * HD + start + width)
        weight = jnp.concatenate([weight_ref[:, rows] for weight_ref in weight_refs], axis=0)
        columns = slice(start, start + width)
        total = dot(grad, weight, 1, 0)
        kept_ref[:, columns] = total[:length]
        sent_ref[:, columns] = total[length:].astype(jnp.bfloat16)


def partial_heads(weights, grad, grad_core, first, count):
    length = grad.shape[0] // 2
    return pl.pallas_call(
        functools.partial(partial_kernel, first, count),
        in_specs=whole(2 + len(weights)),
        out_specs=whole(2),
        out_shape=[
            jax.ShapeDtypeStruct((length, count * HD), jnp.float32),
            jax.ShapeDtypeStruct((length, count * HD), jnp.bfloat16),
        ],
        compiler_params=pltpu.CompilerParams(vmem_limit_bytes=VMEM_LIMIT),
        cost_estimate=SMALL_COST,
        name="partial_heads",
    )(grad, grad_core, *weights)


def columns_kernel(start, stop, wide_ref, *refs):
    (outs_ref, outs_x_ref), arrived, out_ref = refs[:2], refs[2:-1], refs[-1]
    rows = outs_ref.shape[0]
    width = 2 * HD if rows % (2 * HD) == 0 else HD
    for first in range(0, rows, width):
        columns = slice(first, first + width)
        outs = jnp.concatenate([outs_ref[columns], outs_x_ref[columns]], axis=1)
        total = dot(wide_ref[start:stop], outs, 1, 1)
        for arrived_ref in arrived:
            total = total + arrived_ref[start:stop, columns].astype(jnp.float32)
        out_ref[:, columns] = total.astype(out_ref.dtype)


def columns_sum(wide, outs, outs_x, arrived, start, stop, kind):
    rows = outs.shape[0]
    if start % 16 or stop % 16:
        total = dot(wide[start:stop], jnp.concatenate([outs, outs_x], axis=1), 1, 1)
        for piece in arrived:
            total = total + piece[start:stop].astype(jnp.float32)
        return total.astype(kind)
    return pl.pallas_call(
        functools.partial(columns_kernel, start, stop),
        in_specs=whole(3 + len(arrived)),
        out_specs=whole(1)[0],
        out_shape=jax.ShapeDtypeStruct((stop - start, rows), kind),
        compiler_params=pltpu.CompilerParams(vmem_limit_bytes=VMEM_LIMIT),
        cost_estimate=SMALL_COST,
        name="columns_sum",
    )(wide, outs, outs_x, *arrived)


def assemble_kernel(local_heads, firsts, pos_ref, *refs):
    part_refs, (query_ref, key_ref, sems) = refs[:-3], refs[-3:]
    sections = len(part_refs) // len(firsts)
    copies = []
    for index, part_ref in enumerate(part_refs):
        distance, part = index % sections, index // sections
        start = pl.multiple_of(((pos_ref[0] ^ distance) * local_heads + firsts[part]) * HD, HD)
        columns = pl.ds(start, part_ref.shape[2])
        for slot, out_ref in enumerate((query_ref, key_ref)):
            copies.append(
                pltpu.make_async_copy(
                    part_ref.at[slot], out_ref.at[:, columns], sems.at[len(copies)]
                )
            )
    for copy in copies:
        copy.start()
    for copy in copies:
        copy.wait()


def assemble(pos, parts, local_heads, firsts):
    tokens = parts[0].shape[1]
    return pl.pallas_call(
        functools.partial(assemble_kernel, local_heads, firsts),
        in_specs=whole(1, pltpu.SMEM) + whole(len(parts)),
        out_specs=whole(2, pltpu.HBM),
        out_shape=[jax.ShapeDtypeStruct((tokens, HEADS * HD), jnp.bfloat16)] * 2,
        scratch_shapes=[pltpu.SemaphoreType.DMA((2 * len(parts),))],
        compiler_params=pltpu.CompilerParams(vmem_limit_bytes=VMEM_LIMIT),
        cost_estimate=SMALL_COST,
        name="assemble",
    )(pos, *parts)


def add_kernel(*refs):
    out_ref = refs[-1]
    column = 0
    for base_ref, last_ref in zip(refs[:-1:2], refs[1:-1:2]):
        width = base_ref.shape[1]
        out_ref[:, column : column + width] = base_ref[...] + last_ref[...].astype(jnp.float32)
        column += width


def add_parts(pairs):
    rows = pairs[0][0].shape[0]
    width = sum(base.shape[1] for base, _ in pairs)
    return pl.pallas_call(
        add_kernel,
        in_specs=whole(2 * len(pairs)),
        out_specs=whole(1)[0],
        out_shape=jax.ShapeDtypeStruct((rows, width), jnp.float32),
        compiler_params=pltpu.CompilerParams(vmem_limit_bytes=VMEM_LIMIT),
        cost_estimate=SMALL_COST,
        name="add_parts",
    )(*[each for pair in pairs for each in pair])


def bit_reversed(count):
    order = [0]
    while len(order) < count:
        order = [2 * value for value in order] + [2 * value + 1 for value in order]
    return order


def swap_with(array_in, axis_name, distance):
    size = lax.axis_size(axis_name)
    return lax.ppermute(array_in, axis_name, [(i, i ^ distance) for i in range(size)])


def after(array_in, *earlier):
    return lax.optimization_barrier((array_in,) + earlier)[0]


def mask_bits(key_blocks, key_count):
    slots = jnp.arange(key_blocks.shape[2])
    live = slots[None, None, :] < key_count[:, :, None]
    return jnp.sum(jnp.where(live, 1 << key_blocks, 0), axis=2, dtype=jnp.int32)


def split_parts(local_heads):
    if local_heads % 6:
        return (local_heads,)
    return PARTS


def per_device(queries, key_states, value_states, grad_out, out_weight, key_blocks, key_count):
    seq_size = lax.axis_size("seq")
    dp_size = lax.axis_size("dp")
    layers = dp_size // GROUP
    place = lax.axis_index("seq")
    row = lax.axis_index("dp")
    tokens = queries.shape[0]
    local_heads = HEADS // seq_size
    cols = out_weight.shape[1]
    own = (queries, key_states, value_states)
    pos = place.astype(jnp.int32).reshape(1)
    counts = split_parts(local_heads)
    firsts = [sum(counts[:part]) for part in range(len(counts))]
    layer_order = bit_reversed(layers)
    class_cols = layers * cols

    mask = mask_bits(key_blocks, key_count)
    others = range(1, seq_size)
    collected = collect_columns(
        pos, own, local_heads, [(k, firsts[0], counts[0]) for k in others]
    )
    received = [[swap_with(collected[k - 1], "seq", k) for k in others]]

    turned, turned_far = turn_columns(row, after(grad_out, *collected), dp_size)
    grad_x = swap_with(turned_far, "dp", 2)

    shards = {0: after(out_weight, turned).T}
    bit = layers // 2
    while bit:
        for known in sorted(shards):
            shards[known ^ bit] = swap_with(shards[known], "dp", bit * GROUP)
        bit //= 2
    near = [shards[layer] for layer in shards if layer and not layer & (layer - 1)]
    shards = [shards[layer] for layer in layer_order]
    weights = shards + [swap_with(shard, "dp", 1) for shard in shards]
    if cols % 16:
        weights = [jnp.concatenate(weights, axis=0)]

    rest = [(0, firsts[part], counts[part]) for part in range(len(counts))]
    rest += [(k, firsts[part], counts[part]) for part in range(1, len(counts)) for k in others]
    rest = pick_columns(after(pos, turned, mask), own, local_heads, rest)
    own_heads, rest = rest[: len(counts)], rest[len(counts) :]
    for part in range(1, len(counts)):
        sent = rest[(part - 1) * len(others) : part * len(others)]
        received.append([swap_with(after(sent[k - 1], grad_x, *received[part - 1]), "seq", k) for k in others])

    def gather_tokens(dc, *earlier):
        held = after(jnp.stack([turned[dc], grad_x[dc]]), *earlier)
        return [held] + [swap_with(held, "seq", k) for k in others]

    core_pieces = gather_tokens(1, *received[0])
    pieces = gather_tokens(0, *received[-1])

    outs_all, probs_all, outs_x = [], [], []
    for part, count in enumerate(counts):
        outs, probs = attend_forward(
            pos,
            mask,
            [own_heads[part]] + list(received[part]),
            firsts[part],
            count,
            local_heads,
        )
        outs_all.append(outs)
        probs_all.append(probs)
        outs_x.append(swap_with(after(outs, *near) if part else outs, "dp", 2))

    core_wide, core_turned = join_pieces(
        [core_pieces[0]] + [after(piece, outs_all[-1]) for piece in core_pieces[1:]]
    )
    arrived = []
    for part in range(len(counts)):
        if part:
            outs_x[part] = after(outs_x[part], *pieces[1:], *shards)
        sent = columns_sum(
            core_wide, outs_all[part], outs_x[part], [], 0, class_cols, jnp.bfloat16
        )
        arrived.append([swap_with(sent, "dp", 1)])

    grad_wide, grad_turned = join_pieces(
        [pieces[0]] + [after(piece, *[each[0] for each in arrived]) for piece in pieces[1:]]
    )

    def columns_of(part, start, stop, kind):
        return columns_sum(
            grad_wide, outs_all[part], outs_x[part], arrived[part], start, stop, kind
        )

    kept, got, steps = [], [], []
    for part, count in enumerate(counts):
        steps.append([columns_of(part, class_cols // 2, class_cols, jnp.bfloat16)])
        arrived[part].append(swap_with(steps[part][0], "dp", GROUP))
        total, sent = partial_heads(
            weights, after(grad_turned, steps[part][0]), core_turned, firsts[part], count
        )
        kept.append(total)
        got.append(swap_with(sent, "dp", 2))

    weight_parts = []
    for part in range(len(counts)):
        size, bit = class_cols // 2, 1
        while 2 * bit < layers:
            size //= 2
            bit *= 2
            steps[part].append(columns_of(part, size, 2 * size, jnp.bfloat16))
            arrived[part].append(swap_with(steps[part][-1], "dp", bit * GROUP))
        last = arrived[part].pop()
        weight_parts.append((columns_of(part, 0, size, jnp.float32), last))

    back_parts = []
    for part, count in enumerate(counts):
        earlier = [steps[part][-1], steps[-1][0]]
        if part:
            earlier.append(weight_parts[part - 1][1])
        backs = attend_backward(
            [own_heads[part]] + list(received[part]),
            probs_all[part],
            after(kept[part], *earlier),
            got[part],
            count,
        )
        back_parts.append(backs[0])
        back_parts += [swap_with(backs[k], "seq", k) for k in others]
    back_parts[-1] = after(back_parts[-1], steps[-1][-1])
    grad_queries, grad_keys = assemble(pos, back_parts, local_heads, firsts)
    return (grad_queries, grad_keys, add_parts(weight_parts).T)


def solution(mesh):
    return jax.shard_map(
        per_device,
        mesh=mesh,
        in_specs=(
            P(("dp", "seq"), None),
            P(("dp", "seq"), None),
            P(("dp", "seq"), None),
            P(("dp", "seq"), None),
            P("seq", "dp"),
            P(),
            P(),
        ),
        out_specs=(P(("dp", "seq"), None), P(("dp", "seq"), None), P("seq", "dp")),
        check_vma=False,
    )
```

```python
import functools
import math

import jax
import jax.numpy as jnp
from jax import lax
from jax.experimental import pallas as pl
from jax.experimental.pallas import tpu as pltpu
from jax.sharding import PartitionSpec as P

HEADS = 24
HD = 128
BLK = 64
SCALE = HD ** (-0.5)
QUERY_TILE = 256
VMEM_LIMIT = 16 * 1024 * 1024
COLLECT_VMEM = 63 * 1024 * 1024
GROUP = 4
SMALL_COST = pl.CostEstimate(flops=0, bytes_accessed=0, transcendentals=0)
PARTS = (6, 6)


def dot(left, right, left_dim, right_dim):
    return lax.dot_general(
        left, right, (((left_dim,), (right_dim,)), ((), ())), preferred_element_type=jnp.float32
    )


def whole(count, space=pltpu.VMEM):
    return [pl.BlockSpec(memory_space=space)] * count


def mask_rows(mask_ref, place, head, block_total, per_part):
    blocks = [
        (place ^ (block // per_part)) * per_part + block % per_part for block in range(block_total)
    ]
    bits = [mask_ref[head, block] for block in blocks]
    lane = lax.div(lax.broadcasted_iota(jnp.int32, (1, block_total * BLK), 1), jnp.int32(BLK))
    rows = []
    for block in blocks:
        row = jnp.zeros(lane.shape, jnp.float32)
        for query_block in range(block_total):
            allowed = lax.shift_right_logical(bits[query_block], block) & 1
            value = jnp.where(allowed == 1, 0.0, -jnp.inf).astype(jnp.float32)
            row = jnp.where(lane == query_block, value, row)
        rows.append(row)
    return rows


def softmax_columns(key_rows, query_rows, mask, queries):
    scores = dot(key_rows, query_rows, 1, 1) * SCALE
    bias = jnp.concatenate(
        [jnp.broadcast_to(row[:, queries], (BLK, scores.shape[1])) for row in mask], axis=0
    )
    scores = scores + bias
    column_max = jnp.max(scores, axis=0, keepdims=True)
    expo = jnp.exp(scores - column_max)
    return expo * (1.0 / jnp.sum(expo, axis=0, keepdims=True))


def each_head(count, body):
    step = count if count <= 8 else 1

    def run(index, carry):
        for offset in range(step):
            body(index * step + offset)
        return carry

    lax.fori_loop(0, count // step, run, 0)


def head_tokens(piece_refs, columns):
    return [
        jnp.concatenate([piece_ref[slot, :, columns] for piece_ref in piece_refs], axis=0)
        for slot in range(3)
    ]


def column_blocks(width):
    return [slice(low, min(low + 2 * HD, width)) for low in range(0, width, 2 * HD)]


def lanes(head):
    return pl.ds(pl.multiple_of(head * HD, HD), HD)


def forward_kernel(first, count, local_heads, pos_ref, mask_ref, *refs):
    piece_refs, (out_ref, probs_ref) = refs[:-2], refs[-2:]
    length = out_ref.shape[1]
    tokens = length // len(piece_refs)
    tile = min(QUERY_TILE, length)
    place = pos_ref[0]

    def one(head):
        query, key, value = head_tokens(piece_refs, lanes(head))
        mask = mask_rows(
            mask_ref, place, place * local_heads + first + head, length // BLK, tokens // BLK
        )
        for start in range(0, length, tile):
            rows = slice(start, start + tile)
            probs = softmax_columns(key, query[rows], mask, rows)
            probs_ref[head, :, rows] = probs
            out_ref[lanes(head), rows] = dot(value, probs.astype(jnp.bfloat16), 0, 0).astype(
                jnp.bfloat16
            )

    each_head(count, one)


def backward_kernel(count, pieces, *refs):
    piece_refs, (probs_ref, grad_ref, grad_recv_ref) = refs[:pieces], refs[pieces : pieces + 3]
    out_refs = refs[pieces + 3 :]
    length = grad_ref.shape[0]
    tokens = length // pieces
    tile = min(QUERY_TILE, length)

    def one(head):
        columns = lanes(head)
        query, key, value = head_tokens(piece_refs, columns)
        grad_key = None
        for start in range(0, length, tile):
            rows = slice(start, start + tile)
            probs = probs_ref[head, :, rows]
            grad = grad_ref[rows, columns] + grad_recv_ref[rows, columns].astype(jnp.float32)
            dprob = dot(value, grad.astype(jnp.bfloat16), 1, 1)
            delta = jnp.sum(probs * dprob, axis=0, keepdims=True)
            dscore = (probs * (dprob - delta) * SCALE).astype(jnp.bfloat16)
            grad_query = dot(dscore, key, 0, 0).astype(jnp.bfloat16)
            for piece in range(tile // tokens):
                out_refs[start // tokens + piece][0, :, columns] = grad_query[
                    piece * tokens : (piece + 1) * tokens
                ]
            part = dot(dscore, query[rows], 1, 0)
            grad_key = part if grad_key is None else grad_key + part
        grad_key = grad_key.astype(jnp.bfloat16)
        for piece in range(length // tokens):
            out_refs[piece][1, :, columns] = grad_key[piece * tokens : (piece + 1) * tokens]

    each_head(count, one)


def attend_forward(pos, mask, pieces, first, count, local_heads):
    length = pieces[0].shape[1] * len(pieces)
    return pl.pallas_call(
        functools.partial(forward_kernel, first, count, local_heads),
        in_specs=whole(2, pltpu.SMEM) + whole(len(pieces)),
        out_specs=whole(2),
        out_shape=[
            jax.ShapeDtypeStruct((count * HD, length), jnp.bfloat16),
            jax.ShapeDtypeStruct((count, length, length), jnp.float32),
        ],
        compiler_params=pltpu.CompilerParams(vmem_limit_bytes=VMEM_LIMIT),
        cost_estimate=SMALL_COST,
        name="attend_forward",
    )(pos, mask, *pieces)


def attend_backward(pieces, probs, grad, grad_recv, count):
    tokens = pieces[0].shape[1]
    return pl.pallas_call(
        functools.partial(backward_kernel, count, len(pieces)),
        in_specs=whole(3 + len(pieces)),
        out_specs=whole(len(pieces)),
        out_shape=[jax.ShapeDtypeStruct((2, tokens, count * HD), jnp.bfloat16)] * len(pieces),
        compiler_params=pltpu.CompilerParams(vmem_limit_bytes=VMEM_LIMIT),
        cost_estimate=SMALL_COST,
        name="attend_backward",
    )(*pieces, probs, grad, grad_recv)


def collect_kernel(local_heads, pieces, pos_ref, *refs):
    sources, out_refs, sems = refs[:3], refs[3:-1], refs[-1]
    copies = []
    for out_ref, (distance, first, count) in zip(out_refs, pieces):
        start = pl.multiple_of(((pos_ref[0] ^ distance) * local_heads + first) * HD, HD)
        for slot, source in enumerate(sources):
            copies.append(
                pltpu.make_async_copy(
                    source.at[:, pl.ds(start, count * HD)],
                    out_ref.at[slot],
                    sems.at[len(copies)],
                )
            )
    for copy in copies:
        copy.start()
    for copy in copies:
        copy.wait()


def pick_kernel(local_heads, pieces, pos_ref, *refs):
    sources, out_refs = refs[:3], refs[3:]
    for out_ref, (distance, first, count) in zip(out_refs, pieces):
        start = pl.multiple_of(((pos_ref[0] ^ distance) * local_heads + first) * HD, HD)
        for slot, source in enumerate(sources):
            out_ref[slot] = source[:, pl.ds(start, count * HD)]


def pick_columns(pos, sources, local_heads, pieces):
    tokens = sources[0].shape[0]
    return pl.pallas_call(
        functools.partial(pick_kernel, local_heads, pieces),
        in_specs=whole(1, pltpu.SMEM) + whole(len(sources)),
        out_specs=whole(len(pieces)),
        out_shape=[
            jax.ShapeDtypeStruct((len(sources), tokens, count * HD), sources[0].dtype)
            for _, _, count in pieces
        ],
        compiler_params=pltpu.CompilerParams(vmem_limit_bytes=VMEM_LIMIT),
        cost_estimate=SMALL_COST,
        name="pick_columns",
    )(pos, *sources)


def collect_columns(pos, sources, local_heads, pieces):
    tokens = sources[0].shape[0]
    shapes = [(len(sources), tokens, count * HD) for _, _, count in pieces]
    return pl.pallas_call(
        functools.partial(collect_kernel, local_heads, pieces),
        in_specs=whole(1, pltpu.SMEM) + whole(len(sources), pltpu.HBM),
        out_specs=whole(len(pieces)),
        out_shape=[jax.ShapeDtypeStruct(shape, sources[0].dtype) for shape in shapes],
        scratch_shapes=[pltpu.SemaphoreType.DMA((len(sources) * len(pieces),))],
        compiler_params=pltpu.CompilerParams(vmem_limit_bytes=COLLECT_VMEM),
        cost_estimate=SMALL_COST,
        name="collect_columns",
    )(pos, *sources)


def turn_kernel(row_ref, grad_ref, near_ref, far_ref, held_ref):
    blocks, cols, _ = held_ref.shape
    layers = blocks // GROUP
    for block in range(blocks):
        held_ref[block] = grad_ref[:, block * cols : (block + 1) * cols].T
    for dc in range(2):
        for slot, layer in enumerate(bit_reversed(layers)):
            rows = slice(slot * cols, (slot + 1) * cols)
            near_ref[dc, rows] = held_ref[row_ref[0] ^ (GROUP * layer + dc)]
            far_ref[dc, rows] = held_ref[row_ref[0] ^ (GROUP * layer + 2 + dc)]


def turn_columns(row, grad, dp_size):
    tokens, cols = grad.shape[0], grad.shape[1] // dp_size
    layers = dp_size // GROUP
    if cols % 16:
        turned = grad.T.reshape(dp_size, cols, tokens)
        order = [GROUP * layer + kind for kind in range(GROUP) for layer in bit_reversed(layers)]
        turned = jnp.take(turned, row ^ jnp.array(order, jnp.int32), axis=0, mode="clip")
        turned = turned.reshape(2, 2, layers * cols, tokens)
        return turned[0], turned[1]
    return pl.pallas_call(
        turn_kernel,
        in_specs=whole(1, pltpu.SMEM) + whole(1),
        out_specs=whole(2),
        out_shape=[jax.ShapeDtypeStruct((2, layers * cols, tokens), grad.dtype)] * 2,
        scratch_shapes=[pltpu.VMEM((dp_size, cols, tokens), grad.dtype)],
        compiler_params=pltpu.CompilerParams(vmem_limit_bytes=VMEM_LIMIT),
        cost_estimate=SMALL_COST,
        name="turn_columns",
    )(row.astype(jnp.int32).reshape(1), grad)


def join_kernel(*refs):
    piece_refs, wide_ref, turned_ref = refs[:-2], refs[-2], refs[-1]
    tokens = piece_refs[0].shape[2]
    column = 0
    for sequence in range(2):
        for piece_ref in piece_refs:
            piece = piece_ref[sequence]
            wide_ref[:, column : column + tokens] = piece
            turned_ref[column : column + tokens, :] = piece.T
            column += tokens


def join_pieces(pieces):
    _, depth, tokens = pieces[0].shape
    width = 2 * tokens * len(pieces)
    return pl.pallas_call(
        join_kernel,
        in_specs=whole(len(pieces)),
        out_specs=whole(2),
        out_shape=[
            jax.ShapeDtypeStruct((depth, width), jnp.bfloat16),
            jax.ShapeDtypeStruct((width, depth), jnp.bfloat16),
        ],
        compiler_params=pltpu.CompilerParams(vmem_limit_bytes=VMEM_LIMIT),
        cost_estimate=SMALL_COST,
        name="join_pieces",
    )(*pieces)


def partial_kernel(first, grad_ref, grad_core_ref, *refs):
    weight_refs, (kept_ref, sent_ref) = refs[:-2], refs[-2:]
    length, width = kept_ref.shape
    grad = jnp.concatenate([grad_ref[...], grad_core_ref[...]], axis=1)
    for columns in column_blocks(width):
        rows = slice(first * HD + columns.start, first * HD + columns.stop)
        weight = jnp.concatenate(
            [
                weight_ref[:, columns if weight_ref.shape[1] == width else rows]
                for weight_ref in weight_refs
            ],
            axis=0,
        )
        total = dot(grad, weight, 1, 0)
        kept_ref[:, columns] = total[:length]
        sent_ref[:, columns] = total[length:].astype(jnp.bfloat16)


def partial_heads(weights, grad, grad_core, first, count):
    length = grad.shape[0] // 2
    return pl.pallas_call(
        functools.partial(partial_kernel, first),
        in_specs=whole(2 + len(weights)),
        out_specs=whole(2),
        out_shape=[
            jax.ShapeDtypeStruct((length, count * HD), jnp.float32),
            jax.ShapeDtypeStruct((length, count * HD), jnp.bfloat16),
        ],
        compiler_params=pltpu.CompilerParams(vmem_limit_bytes=VMEM_LIMIT),
        cost_estimate=SMALL_COST,
        name="partial_heads",
    )(grad, grad_core, *weights)


def columns_kernel(start, stop, starts, wide_ref, outs_ref, outs_x_ref, *refs):
    arrived_refs, out_ref = refs[:-1], refs[-1]
    bounds = {start, stop}
    for arrived_ref, first in zip(arrived_refs, starts):
        bounds |= {edge for edge in (first, first + arrived_ref.shape[0]) if start < edge < stop}
    bounds = sorted(bounds)
    for columns in column_blocks(outs_ref.shape[0]):
        outs = jnp.concatenate([outs_ref[columns], outs_x_ref[columns]], axis=1)
        for low, high in zip(bounds[:-1], bounds[1:]):
            total = dot(wide_ref[low:high], outs, 1, 1)
            for arrived_ref, first in zip(arrived_refs, starts):
                if first <= low and high <= first + arrived_ref.shape[0]:
                    rows = slice(low - first, high - first)
                    total = total + arrived_ref[rows, columns].astype(jnp.float32)
            out_ref[low - start : high - start, columns] = total.astype(out_ref.dtype)


def columns_sum(wide, outs, outs_x, arrived, start, stop, kind):
    rows = outs.shape[0]
    arrived = [(p, first) for p, first in arrived if first < stop and start < first + p.shape[0]]
    if start % 16 or stop % 16:
        total = dot(wide[start:stop], jnp.concatenate([outs, outs_x], axis=1), 1, 1)
        for piece, first in arrived:
            low, high = max(start, first), min(stop, first + piece.shape[0])
            part = piece[low - first : high - first].astype(jnp.float32)
            total = total + jnp.pad(part, ((low - start, stop - high), (0, 0)))
        return total.astype(kind)
    return pl.pallas_call(
        functools.partial(columns_kernel, start, stop, [first for _, first in arrived]),
        in_specs=whole(3 + len(arrived)),
        out_specs=whole(1)[0],
        out_shape=jax.ShapeDtypeStruct((stop - start, rows), kind),
        compiler_params=pltpu.CompilerParams(vmem_limit_bytes=VMEM_LIMIT),
        cost_estimate=SMALL_COST,
        name="columns_sum",
    )(wide, outs, outs_x, *[piece for piece, _ in arrived])


def assemble_kernel(local_heads, firsts, pos_ref, *refs):
    part_refs, (query_ref, key_ref, sems) = refs[:-3], refs[-3:]
    sections = len(part_refs) // len(firsts)
    copies = []
    for index, part_ref in enumerate(part_refs):
        distance, part = index % sections, index // sections
        start = pl.multiple_of(((pos_ref[0] ^ distance) * local_heads + firsts[part]) * HD, HD)
        columns = pl.ds(start, part_ref.shape[2])
        for slot, out_ref in enumerate((query_ref, key_ref)):
            copies.append(
                pltpu.make_async_copy(
                    part_ref.at[slot], out_ref.at[:, columns], sems.at[len(copies)]
                )
            )
    for copy in copies:
        copy.start()
    for copy in copies:
        copy.wait()


def assemble(pos, parts, local_heads, firsts):
    tokens = parts[0].shape[1]
    return pl.pallas_call(
        functools.partial(assemble_kernel, local_heads, firsts),
        in_specs=whole(1, pltpu.SMEM) + whole(len(parts)),
        out_specs=whole(2, pltpu.HBM),
        out_shape=[jax.ShapeDtypeStruct((tokens, HEADS * HD), jnp.bfloat16)] * 2,
        scratch_shapes=[pltpu.SemaphoreType.DMA((2 * len(parts),))],
        compiler_params=pltpu.CompilerParams(vmem_limit_bytes=VMEM_LIMIT),
        cost_estimate=SMALL_COST,
        name="assemble",
    )(pos, *parts)


def add_kernel(*refs):
    out_ref = refs[-1]
    column = 0
    for base_ref, last_ref in zip(refs[:-1:2], refs[1:-1:2]):
        width = base_ref.shape[1]
        out_ref[:, column : column + width] = base_ref[...] + last_ref[...].astype(jnp.float32)
        column += width


def add_parts(pairs):
    rows = pairs[0][0].shape[0]
    width = sum(base.shape[1] for base, _ in pairs)
    return pl.pallas_call(
        add_kernel,
        in_specs=whole(2 * len(pairs)),
        out_specs=whole(1)[0],
        out_shape=jax.ShapeDtypeStruct((rows, width), jnp.float32),
        compiler_params=pltpu.CompilerParams(vmem_limit_bytes=VMEM_LIMIT),
        cost_estimate=SMALL_COST,
        name="add_parts",
    )(*[each for pair in pairs for each in pair])


def bit_reversed(count):
    order = [0]
    while len(order) < count:
        order = [2 * value for value in order] + [2 * value + 1 for value in order]
    return order


def swap_with(array_in, axis_name, distance):
    size = lax.axis_size(axis_name)
    return lax.ppermute(array_in, axis_name, [(i, i ^ distance) for i in range(size)])


def after(array_in, *earlier):
    return lax.optimization_barrier((array_in,) + earlier)[0]


def mask_bits(key_blocks, key_count):
    slots = jnp.arange(key_blocks.shape[2])
    live = slots[None, None, :] < key_count[:, :, None]
    return jnp.sum(jnp.where(live, 1 << key_blocks, 0), axis=2, dtype=jnp.int32)


def split_parts(local_heads):
    if local_heads % 6:
        return (local_heads,)
    return PARTS


def per_device(queries, key_states, value_states, grad_out, out_weight, key_blocks, key_count):
    seq_size = lax.axis_size("seq")
    dp_size = lax.axis_size("dp")
    layers = dp_size // GROUP
    place = lax.axis_index("seq")
    row = lax.axis_index("dp")
    tokens = queries.shape[0]
    local_heads = HEADS // seq_size
    cols = out_weight.shape[1]
    own = (queries, key_states, value_states)
    pos = place.astype(jnp.int32).reshape(1)
    counts = split_parts(local_heads)
    firsts = [sum(counts[:part]) for part in range(len(counts))]
    layer_order = bit_reversed(layers)
    class_cols = layers * cols

    mask = mask_bits(key_blocks, key_count)
    others = range(1, seq_size)
    collected = collect_columns(
        pos, own, local_heads, [(k, firsts[0], counts[0]) for k in others]
    )
    received = [[swap_with(collected[k - 1], "seq", k) for k in others]]

    turned, turned_far = turn_columns(row, after(grad_out, *collected), dp_size)
    grad_x = swap_with(turned_far, "dp", 2)

    shards = {0: after(out_weight, turned).T}
    bits = [1 << power for power in reversed(range(layers.bit_length() - 1))]
    for bit in bits:
        shards[bit] = swap_with(shards[0], "dp", bit * GROUP)

    rest = [(0, firsts[part], counts[part]) for part in range(len(counts))]
    rest += [(k, firsts[part], counts[part]) for part in range(1, len(counts)) for k in others]
    rest = pick_columns(after(pos, turned, mask), own, local_heads, rest)
    own_heads, rest = rest[: len(counts)], rest[len(counts) :]
    for part in range(1, len(counts)):
        sent = rest[(part - 1) * len(others) : part * len(others)]
        received.append(
            [swap_with(after(sent[k - 1], grad_x, *received[part - 1]), "seq", k) for k in others]
        )

    def swap_core(part, layer, *earlier):
        rows = slice(firsts[part] * HD, (firsts[part] + counts[part]) * HD)
        shard = after(shards[layer], *earlier) if earlier else shards[layer]
        core_shards[part][layer] = swap_with(shard[:, rows], "dp", 1)

    core_shards = [{} for _ in counts]
    for part in range(len(counts)):
        swap_core(part, 0)
    own_core = [each[0] for each in core_shards]
    outs_all, probs_all, outs_x = [], [], []
    for part, count in enumerate(counts):
        outs, probs = attend_forward(
            pos,
            mask,
            [after(own_heads[part], *own_core)] + list(received[part]),
            firsts[part],
            count,
            local_heads,
        )
        outs_all.append(outs)
        probs_all.append(probs)
        outs_x.append(swap_with(outs, "dp", 2))
    for layer in bits:
        swap_core(0, layer, outs_all[0])
    near = [core_shards[0][layer] for layer in bits]
    for bit in bits:
        for known in sorted(shards):
            if known & (bit - 1) == 0 and known ^ bit not in shards:
                shards[known ^ bit] = swap_with(
                    after(shards[known], outs_all[0]), "dp", bit * GROUP
                )
    for part in range(len(counts)):
        for layer in layer_order:
            if layer not in core_shards[part]:
                swap_core(part, layer)
    shards = [shards[layer] for layer in layer_order]

    def weights_of(part):
        rows = slice(firsts[part] * HD, (firsts[part] + counts[part]) * HD)
        core = [core_shards[part][layer] for layer in layer_order]
        if cols % 16:
            return [jnp.concatenate([shard[:, rows] for shard in shards] + core, axis=0)]
        return shards + core

    def gather_tokens(dc, *earlier):
        held = after(jnp.stack([turned[dc], grad_x[dc]]), *earlier)
        return [held] + [swap_with(held, "seq", k) for k in others]

    core_pieces = gather_tokens(1, *received[-1], *near)
    pieces = gather_tokens(0, *received[-1])

    core_pieces[1:] = [after(piece, outs_all[-1]) for piece in core_pieces[1:]]
    core_wide, core_turned = join_pieces(core_pieces)
    arrived = [[] for _ in counts]
    quarter = class_cols // 4

    def send_core(part, start, stop, *earlier):
        sent = columns_sum(
            after(core_wide, *earlier) if earlier else core_wide,
            outs_all[part],
            outs_x[part],
            [],
            start * quarter,
            stop * quarter,
            jnp.bfloat16,
        )
        arrived[part].append((swap_with(sent, "dp", 1), start * quarter))

    send_core(0, 3, 4)
    send_core(0, 2, 3)
    for part in range(1, len(counts)):
        send_core(part, 2, 4)

    pieces[1:] = [after(piece, *shards) for piece in pieces[1:]]
    grad_wide, grad_turned = join_pieces(pieces)

    def columns_of(part, start, stop, kind, *earlier):
        outs = after(outs_all[part], *earlier) if earlier else outs_all[part]
        return columns_sum(grad_wide, outs, outs_x[part], arrived[part], start, stop, kind)

    kept, got, last = [], [], []
    for part, count in enumerate(counts):
        sent = columns_of(part, quarter * 2, quarter * 4, jnp.bfloat16, *last)
        arrived[part].append((swap_with(sent, "dp", GROUP), 0))
        total, sent = partial_heads(
            weights_of(part), after(grad_turned, sent), core_turned, firsts[part], count
        )
        kept.append(total)
        got.append(swap_with(sent, "dp", 2))
        last = [total]
        send_core(part, 0, 2, total)

    weight_parts, back_parts = [], []
    for part, count in enumerate(counts):
        size = class_cols // 2

        def next_sums(last):
            size = class_cols // 2
            for bit in [1 << power for power in range(1, layers.bit_length() - 1)]:
                size //= 2
                sent = columns_of(part, size, 2 * size, jnp.bfloat16, *last)
                arrived[part].append((swap_with(sent, "dp", bit * GROUP), 0))
                last = [sent]
            return last

        if part == 0:
            last = next_sums(last)
        backs = attend_backward(
            [own_heads[part]] + list(received[part]),
            probs_all[part],
            after(kept[part], *last),
            got[part],
            count,
        )
        last = [backs[0]]
        back_parts.append(backs[0])
        back_parts += [swap_with(backs[k], "seq", k) for k in others]
        if part:
            last = next_sums(last + [arrived[0][-1][0]])
    for part in range(len(counts)):
        final, _ = arrived[part].pop()
        weight_parts.append((columns_of(part, 0, cols, jnp.float32, *last), final))
    grad_queries, grad_keys = assemble(pos, back_parts, local_heads, firsts)
    return (grad_queries, grad_keys, add_parts(weight_parts).T)


def solution(mesh):
    return jax.shard_map(
        per_device,
        mesh=mesh,
        in_specs=(
            P(("dp", "seq"), None),
            P(("dp", "seq"), None),
            P(("dp", "seq"), None),
            P(("dp", "seq"), None),
            P("seq", "dp"),
            P(),
            P(),
        ),
        out_specs=(P(("dp", "seq"), None), P(("dp", "seq"), None), P("seq", "dp")),
        check_vma=False,
    )
```

```python
import functools
import math

import jax
import jax.numpy as jnp
from jax import lax
from jax.experimental import pallas as pl
from jax.experimental.pallas import tpu as pltpu
from jax.sharding import PartitionSpec as P

HEADS = 24
HD = 128
BLK = 64
SCALE = HD ** (-0.5)
QUERY_TILE = 256
VMEM_LIMIT = 16 * 1024 * 1024
COLLECT_VMEM = 63 * 1024 * 1024
GROUP = 4
FIRST_COST = pl.CostEstimate(flops=3500000000, bytes_accessed=0, transcendentals=0)
LAST_COST = pl.CostEstimate(flops=1200000000, bytes_accessed=0, transcendentals=0)
SMALL_COST = pl.CostEstimate(flops=0, bytes_accessed=0, transcendentals=0)
PARTS = (8, 4)


def dot(left, right, left_dim, right_dim):
    return lax.dot_general(
        left, right, (((left_dim,), (right_dim,)), ((), ())), preferred_element_type=jnp.float32
    )


def whole(count, space=pltpu.VMEM):
    return [pl.BlockSpec(memory_space=space)] * count


def mask_rows(mask_ref, place, head, block_total, per_part):
    blocks = [
        (place ^ (block // per_part)) * per_part + block % per_part for block in range(block_total)
    ]
    bits = [mask_ref[head, block] for block in blocks]
    lane = lax.div(lax.broadcasted_iota(jnp.int32, (1, block_total * BLK), 1), jnp.int32(BLK))
    rows = []
    for block in blocks:
        row = jnp.zeros(lane.shape, jnp.float32)
        for query_block in range(block_total):
            allowed = lax.shift_right_logical(bits[query_block], block) & 1
            value = jnp.where(allowed == 1, 0.0, -jnp.inf).astype(jnp.float32)
            row = jnp.where(lane == query_block, value, row)
        rows.append(row)
    return rows


def softmax_columns(key_rows, query_rows, mask, queries):
    scores = dot(key_rows, query_rows, 1, 1) * SCALE
    bias = jnp.concatenate(
        [jnp.broadcast_to(row[:, queries], (BLK, scores.shape[1])) for row in mask], axis=0
    )
    scores = scores + bias
    column_max = jnp.max(scores, axis=0, keepdims=True)
    expo = jnp.exp(scores - column_max)
    return expo * (1.0 / jnp.sum(expo, axis=0, keepdims=True))


def each_head(count, body):
    step = count if count <= 8 else 1

    def run(index, carry):
        for offset in range(step):
            body(index * step + offset)
        return carry

    lax.fori_loop(0, count // step, run, 0)


def head_tokens(piece_refs, columns):
    return [
        jnp.concatenate([piece_ref[slot, :, columns] for piece_ref in piece_refs], axis=0)
        for slot in range(3)
    ]


def column_blocks(width):
    return [slice(low, min(low + 2 * HD, width)) for low in range(0, width, 2 * HD)]


def lanes(head):
    return pl.ds(pl.multiple_of(head * HD, HD), HD)


def forward_kernel(first, count, local_heads, pos_ref, mask_ref, *refs):
    piece_refs, (out_ref, probs_ref) = refs[:-2], refs[-2:]
    length = out_ref.shape[1]
    tokens = length // len(piece_refs)
    tile = min(QUERY_TILE, length)
    place = pos_ref[0]

    def one(head):
        query, key, value = head_tokens(piece_refs, lanes(head))
        mask = mask_rows(
            mask_ref, place, place * local_heads + first + head, length // BLK, tokens // BLK
        )
        for start in range(0, length, tile):
            rows = slice(start, start + tile)
            probs = softmax_columns(key, query[rows], mask, rows)
            probs_ref[head, :, rows] = probs
            out_ref[lanes(head), rows] = dot(value, probs.astype(jnp.bfloat16), 0, 0).astype(
                jnp.bfloat16
            )

    each_head(count, one)


def backward_kernel(count, pieces, *refs):
    piece_refs, (probs_ref, grad_ref, grad_recv_ref) = refs[:pieces], refs[pieces : pieces + 3]
    out_refs = refs[pieces + 3 :]
    length = grad_ref.shape[0]
    tokens = length // pieces
    tile = min(QUERY_TILE, length)

    def one(head):
        columns = lanes(head)
        query, key, value = head_tokens(piece_refs, columns)
        grad_key = None
        for start in range(0, length, tile):
            rows = slice(start, start + tile)
            probs = probs_ref[head, :, rows]
            grad = grad_ref[rows, columns] + grad_recv_ref[rows, columns].astype(jnp.float32)
            dprob = dot(value, grad.astype(jnp.bfloat16), 1, 1)
            delta = jnp.sum(probs * dprob, axis=0, keepdims=True)
            dscore = (probs * (dprob - delta) * SCALE).astype(jnp.bfloat16)
            grad_query = dot(dscore, key, 0, 0).astype(jnp.bfloat16)
            for piece in range(tile // tokens):
                out_refs[start // tokens + piece][0, :, columns] = grad_query[
                    piece * tokens : (piece + 1) * tokens
                ]
            part = dot(dscore, query[rows], 1, 0)
            grad_key = part if grad_key is None else grad_key + part
        grad_key = grad_key.astype(jnp.bfloat16)
        for piece in range(length // tokens):
            out_refs[piece][1, :, columns] = grad_key[piece * tokens : (piece + 1) * tokens]

    each_head(count, one)


def attend_forward(pos, mask, pieces, first, count, local_heads):
    length = pieces[0].shape[1] * len(pieces)
    return pl.pallas_call(
        functools.partial(forward_kernel, first, count, local_heads),
        in_specs=whole(2, pltpu.SMEM) + whole(len(pieces)),
        out_specs=whole(2),
        out_shape=[
            jax.ShapeDtypeStruct((count * HD, length), jnp.bfloat16),
            jax.ShapeDtypeStruct((count, length, length), jnp.float32),
        ],
        compiler_params=pltpu.CompilerParams(vmem_limit_bytes=VMEM_LIMIT),
        cost_estimate=SMALL_COST,
        name="attend_forward",
    )(pos, mask, *pieces)


def attend_backward(pieces, probs, grad, grad_recv, count, cost):
    tokens = pieces[0].shape[1]
    return pl.pallas_call(
        functools.partial(backward_kernel, count, len(pieces)),
        in_specs=whole(3 + len(pieces)),
        out_specs=whole(len(pieces)),
        out_shape=[jax.ShapeDtypeStruct((2, tokens, count * HD), jnp.bfloat16)] * len(pieces),
        compiler_params=pltpu.CompilerParams(vmem_limit_bytes=VMEM_LIMIT),
        cost_estimate=cost,
        name="attend_backward",
    )(*pieces, probs, grad, grad_recv)


def collect_kernel(local_heads, pieces, pos_ref, *refs):
    sources, out_refs, sems = refs[:3], refs[3:-1], refs[-1]
    copies = []
    for out_ref, (distance, first, count) in zip(out_refs, pieces):
        start = pl.multiple_of(((pos_ref[0] ^ distance) * local_heads + first) * HD, HD)
        for slot, source in enumerate(sources):
            copies.append(
                pltpu.make_async_copy(
                    source.at[:, pl.ds(start, count * HD)],
                    out_ref.at[slot],
                    sems.at[len(copies)],
                )
            )
    for copy in copies:
        copy.start()
    for copy in copies:
        copy.wait()


def pick_kernel(local_heads, pieces, pos_ref, *refs):
    sources, out_refs = refs[:3], refs[3:]
    for out_ref, (distance, first, count) in zip(out_refs, pieces):
        start = pl.multiple_of(((pos_ref[0] ^ distance) * local_heads + first) * HD, HD)
        for slot, source in enumerate(sources):
            out_ref[slot] = source[:, pl.ds(start, count * HD)]


def pick_columns(pos, sources, local_heads, pieces):
    tokens = sources[0].shape[0]
    return pl.pallas_call(
        functools.partial(pick_kernel, local_heads, pieces),
        in_specs=whole(1, pltpu.SMEM) + whole(len(sources)),
        out_specs=whole(len(pieces)),
        out_shape=[
            jax.ShapeDtypeStruct((len(sources), tokens, count * HD), sources[0].dtype)
            for _, _, count in pieces
        ],
        compiler_params=pltpu.CompilerParams(vmem_limit_bytes=VMEM_LIMIT),
        cost_estimate=SMALL_COST,
        name="pick_columns",
    )(pos, *sources)


def collect_columns(pos, sources, local_heads, pieces):
    tokens = sources[0].shape[0]
    shapes = [(len(sources), tokens, count * HD) for _, _, count in pieces]
    return pl.pallas_call(
        functools.partial(collect_kernel, local_heads, pieces),
        in_specs=whole(1, pltpu.SMEM) + whole(len(sources), pltpu.HBM),
        out_specs=whole(len(pieces)),
        out_shape=[jax.ShapeDtypeStruct(shape, sources[0].dtype) for shape in shapes],
        scratch_shapes=[pltpu.SemaphoreType.DMA((len(sources) * len(pieces),))],
        compiler_params=pltpu.CompilerParams(vmem_limit_bytes=COLLECT_VMEM),
        cost_estimate=SMALL_COST,
        name="collect_columns",
    )(pos, *sources)


def turn_kernel(row_ref, grad_ref, near_ref, far_ref, held_ref):
    blocks, cols, _ = held_ref.shape
    layers = blocks // GROUP
    for block in range(blocks):
        held_ref[block] = grad_ref[:, block * cols : (block + 1) * cols].T
    for dc in range(2):
        for slot, layer in enumerate(bit_reversed(layers)):
            first = (dc * layers + slot) * cols
            rows = slice(first, first + cols)
            near_ref[rows] = held_ref[row_ref[0] ^ (GROUP * layer + dc)]
            far_ref[rows] = held_ref[row_ref[0] ^ (GROUP * layer + 2 + dc)]


def turn_columns(row, grad, dp_size):
    tokens, cols = grad.shape[0], grad.shape[1] // dp_size
    layers = dp_size // GROUP
    if cols % 16:
        turned = grad.T.reshape(dp_size, cols, tokens)
        order = [GROUP * layer + kind for kind in range(GROUP) for layer in bit_reversed(layers)]
        turned = jnp.take(turned, row ^ jnp.array(order, jnp.int32), axis=0, mode="clip")
        turned = turned.reshape(2, 2 * layers * cols, tokens)
        return turned[0], turned[1]
    return pl.pallas_call(
        turn_kernel,
        in_specs=whole(1, pltpu.SMEM) + whole(1),
        out_specs=whole(2),
        out_shape=[jax.ShapeDtypeStruct((2 * layers * cols, tokens), grad.dtype)] * 2,
        scratch_shapes=[pltpu.VMEM((dp_size, cols, tokens), grad.dtype)],
        compiler_params=pltpu.CompilerParams(vmem_limit_bytes=VMEM_LIMIT),
        cost_estimate=SMALL_COST,
        name="turn_columns",
    )(row.astype(jnp.int32).reshape(1), grad)


def join_kernel(*refs):
    piece_refs, wide_ref, turned_ref = refs[:-2], refs[-2], refs[-1]
    tokens = piece_refs[0].shape[2]
    column = 0
    for sequence in range(2):
        for piece_ref in piece_refs:
            piece = piece_ref[sequence]
            wide_ref[:, column : column + tokens] = piece
            turned_ref[column : column + tokens, :] = piece.T
            column += tokens


def join_pieces(pieces):
    _, depth, tokens = pieces[0].shape
    width = 2 * tokens * len(pieces)
    return pl.pallas_call(
        join_kernel,
        in_specs=whole(len(pieces)),
        out_specs=whole(2),
        out_shape=[
            jax.ShapeDtypeStruct((depth, width), jnp.bfloat16),
            jax.ShapeDtypeStruct((width, depth), jnp.bfloat16),
        ],
        compiler_params=pltpu.CompilerParams(vmem_limit_bytes=VMEM_LIMIT),
        cost_estimate=SMALL_COST,
        name="join_pieces",
    )(*pieces)


def partial_kernel(first, grad_ref, *refs):
    weight_refs, (kept_ref, sent_ref) = refs[:-2], refs[-2:]
    length, width = kept_ref.shape
    for columns in column_blocks(width):
        rows = slice(first * HD + columns.start, first * HD + columns.stop)
        weight = jnp.concatenate(
            [
                weight_ref[:, columns if weight_ref.shape[1] == width else rows]
                for weight_ref in weight_refs
            ],
            axis=0,
        )
        total = dot(grad_ref[...], weight, 1, 0)
        kept_ref[:, columns] = total[:length]
        sent_ref[:, columns] = total[length:].astype(jnp.bfloat16)


def partial_heads(weights, grad, first, count):
    length = grad.shape[0] // 2
    return pl.pallas_call(
        functools.partial(partial_kernel, first),
        in_specs=whole(1 + len(weights)),
        out_specs=whole(2),
        out_shape=[
            jax.ShapeDtypeStruct((length, count * HD), jnp.float32),
            jax.ShapeDtypeStruct((length, count * HD), jnp.bfloat16),
        ],
        compiler_params=pltpu.CompilerParams(vmem_limit_bytes=VMEM_LIMIT),
        cost_estimate=SMALL_COST,
        name="partial_heads",
    )(grad, *weights)


def columns_kernel(start, stop, starts, wide_ref, outs_ref, outs_x_ref, *refs):
    arrived_refs, out_ref = refs[:-1], refs[-1]
    bounds = {start, stop}
    for arrived_ref, first in zip(arrived_refs, starts):
        bounds |= {edge for edge in (first, first + arrived_ref.shape[0]) if start < edge < stop}
    bounds = sorted(bounds)
    for columns in column_blocks(outs_ref.shape[0]):
        outs = jnp.concatenate([outs_ref[columns], outs_x_ref[columns]], axis=1)
        for low, high in zip(bounds[:-1], bounds[1:]):
            total = dot(wide_ref[low:high], outs, 1, 1)
            for arrived_ref, first in zip(arrived_refs, starts):
                if first <= low and high <= first + arrived_ref.shape[0]:
                    rows = slice(low - first, high - first)
                    total = total + arrived_ref[rows, columns].astype(jnp.float32)
            out_ref[low - start : high - start, columns] = total.astype(out_ref.dtype)


def columns_sum(wide, outs, outs_x, arrived, start, stop, kind, cost=SMALL_COST):
    rows = outs.shape[0]
    arrived = [(p, first) for p, first in arrived if first < stop and start < first + p.shape[0]]
    if start % 16 or stop % 16:
        total = dot(wide[start:stop], jnp.concatenate([outs, outs_x], axis=1), 1, 1)
        for piece, first in arrived:
            low, high = max(start, first), min(stop, first + piece.shape[0])
            part = piece[low - first : high - first].astype(jnp.float32)
            total = total + jnp.pad(part, ((low - start, stop - high), (0, 0)))
        return total.astype(kind)
    return pl.pallas_call(
        functools.partial(columns_kernel, start, stop, [first for _, first in arrived]),
        in_specs=whole(3 + len(arrived)),
        out_specs=whole(1)[0],
        out_shape=jax.ShapeDtypeStruct((stop - start, rows), kind),
        compiler_params=pltpu.CompilerParams(vmem_limit_bytes=VMEM_LIMIT),
        cost_estimate=cost,
        name="columns_sum",
    )(wide, outs, outs_x, *[piece for piece, _ in arrived])


def assemble_kernel(local_heads, firsts, pos_ref, *refs):
    part_refs, (query_ref, key_ref, sems) = refs[:-3], refs[-3:]
    sections = len(part_refs) // len(firsts)
    copies = []
    for index, part_ref in enumerate(part_refs):
        distance, part = index % sections, index // sections
        start = pl.multiple_of(((pos_ref[0] ^ distance) * local_heads + firsts[part]) * HD, HD)
        columns = pl.ds(start, part_ref.shape[2])
        for slot, out_ref in enumerate((query_ref, key_ref)):
            copies.append(
                pltpu.make_async_copy(
                    part_ref.at[slot], out_ref.at[:, columns], sems.at[len(copies)]
                )
            )
    for copy in copies:
        copy.start()
    for copy in copies:
        copy.wait()


def assemble(pos, parts, local_heads, firsts):
    tokens = parts[0].shape[1]
    return pl.pallas_call(
        functools.partial(assemble_kernel, local_heads, firsts),
        in_specs=whole(1, pltpu.SMEM) + whole(len(parts)),
        out_specs=whole(2, pltpu.HBM),
        out_shape=[jax.ShapeDtypeStruct((tokens, HEADS * HD), jnp.bfloat16)] * 2,
        scratch_shapes=[pltpu.SemaphoreType.DMA((2 * len(parts),))],
        compiler_params=pltpu.CompilerParams(vmem_limit_bytes=VMEM_LIMIT),
        cost_estimate=SMALL_COST,
        name="assemble",
    )(pos, *parts)


def add_kernel(*refs):
    out_ref = refs[-1]
    column = 0
    for base_ref, last_ref in zip(refs[:-1:2], refs[1:-1:2]):
        width = base_ref.shape[1]
        out_ref[:, column : column + width] = base_ref[...] + last_ref[...].astype(jnp.float32)
        column += width


def add_parts(pairs):
    rows = pairs[0][0].shape[0]
    width = sum(base.shape[1] for base, _ in pairs)
    return pl.pallas_call(
        add_kernel,
        in_specs=whole(2 * len(pairs)),
        out_specs=whole(1)[0],
        out_shape=jax.ShapeDtypeStruct((rows, width), jnp.float32),
        compiler_params=pltpu.CompilerParams(vmem_limit_bytes=VMEM_LIMIT),
        cost_estimate=SMALL_COST,
        name="add_parts",
    )(*[each for pair in pairs for each in pair])


def bit_reversed(count):
    order = [0]
    while len(order) < count:
        order = [2 * value for value in order] + [2 * value + 1 for value in order]
    return order


def swap_with(array_in, axis_name, distance):
    size = lax.axis_size(axis_name)
    return lax.ppermute(array_in, axis_name, [(i, i ^ distance) for i in range(size)])


def after(array_in, *earlier):
    return lax.optimization_barrier((array_in,) + earlier)[0]


def mask_bits(key_blocks, key_count):
    slots = jnp.arange(key_blocks.shape[2])
    live = slots[None, None, :] < key_count[:, :, None]
    return jnp.sum(jnp.where(live, 1 << key_blocks, 0), axis=2, dtype=jnp.int32)


def split_parts(local_heads):
    if local_heads % 6:
        return (local_heads,)
    return PARTS


def per_device(queries, key_states, value_states, grad_out, out_weight, key_blocks, key_count):
    seq_size = lax.axis_size("seq")
    dp_size = lax.axis_size("dp")
    layers = dp_size // GROUP
    place = lax.axis_index("seq")
    row = lax.axis_index("dp")
    tokens = queries.shape[0]
    local_heads = HEADS // seq_size
    cols = out_weight.shape[1]
    own = (queries, key_states, value_states)
    pos = place.astype(jnp.int32).reshape(1)
    counts = split_parts(local_heads)
    firsts = [sum(counts[:part]) for part in range(len(counts))]
    layer_order = bit_reversed(layers)
    class_cols = layers * cols

    mask = mask_bits(key_blocks, key_count)
    others = range(1, seq_size)
    collected = collect_columns(
        pos, own, local_heads, [(k, firsts[0], counts[0]) for k in others]
    )
    received = [[swap_with(collected[k - 1], "seq", k) for k in others]]

    turned, turned_far = turn_columns(row, after(grad_out, *collected), dp_size)
    grad_x = swap_with(turned_far, "dp", 2)

    shards = {0: after(out_weight, turned).T}
    bits = [1 << power for power in reversed(range(layers.bit_length() - 1))]
    for bit in bits:
        shards[bit] = swap_with(shards[0], "dp", bit * GROUP)

    rest = [(0, firsts[part], counts[part]) for part in range(len(counts))]
    rest += [(k, firsts[part], counts[part]) for part in range(1, len(counts)) for k in others]
    rest = pick_columns(after(pos, turned, mask), own, local_heads, rest)
    own_heads, rest = rest[: len(counts)], rest[len(counts) :]
    held = after(jnp.stack([turned, grad_x]), *received[0], *own_heads)
    pieces = [held] + [swap_with(held, "seq", k) for k in others]
    for part in range(1, len(counts)):
        sent = rest[(part - 1) * len(others) : part * len(others)]
        received.append(
            [swap_with(after(sent[k - 1], *pieces[1:]), "seq", k) for k in others]
        )

    def swap_core(part, layer, *earlier):
        rows = slice(firsts[part] * HD, (firsts[part] + counts[part]) * HD)
        shard = after(shards[layer], *earlier) if earlier else shards[layer]
        core_shards[part][layer] = swap_with(shard[:, rows], "dp", 1)

    core_shards = [{} for _ in counts]
    for part in range(len(counts)):
        swap_core(part, 0)
    own_core = [each[0] for each in core_shards]
    outs_all, probs_all, outs_x = [], [], []

    def forward(part, *earlier):
        outs, probs = attend_forward(
            pos,
            mask,
            [after(own_heads[part], own_core[part], *earlier)] + list(received[part]),
            firsts[part],
            counts[part],
            local_heads,
        )
        outs_all.append(outs)
        probs_all.append(probs)
        outs_x.append(swap_with(outs, "dp", 2))

    forward(0)
    for layer in bits:
        swap_core(0, layer, outs_all[0])
    near = [core_shards[0][layer] for layer in bits]
    for bit in bits:
        for known in sorted(shards):
            if known & (bit - 1) == 0 and known ^ bit not in shards:
                shards[known ^ bit] = swap_with(
                    after(shards[known], outs_all[0]), "dp", bit * GROUP
                )
    for part in range(len(counts)):
        for layer in layer_order:
            if layer not in core_shards[part]:
                swap_core(part, layer)
    shards = [shards[layer] for layer in layer_order]

    def weights_of(part):
        rows = slice(firsts[part] * HD, (firsts[part] + counts[part]) * HD)
        core = [core_shards[part][layer] for layer in layer_order]
        if cols % 16:
            return [jnp.concatenate([shard[:, rows] for shard in shards] + core, axis=0)]
        return shards + core

    pieces[1:] = [after(piece, *near) for piece in pieces[1:]]
    grad_wide, grad_turned = join_pieces(pieces)
    arrived = [[] for _ in counts]
    half = class_cols // 2

    def send_core(part, start, stop, *earlier):
        sent = columns_sum(
            after(grad_wide, *earlier) if earlier else grad_wide,
            outs_all[part],
            outs_x[part],
            [],
            class_cols + start,
            class_cols + stop,
            jnp.bfloat16,
        )
        arrived[part].append((swap_with(sent, "dp", 1), start))

    for start in range(half, class_cols, half // 2):
        send_core(0, start, start + half // 2)

    def columns_of(part, start, stop, kind, *earlier, cost=SMALL_COST):
        outs = after(outs_all[part], *earlier) if earlier else outs_all[part]
        return columns_sum(grad_wide, outs, outs_x[part], arrived[part], start, stop, kind, cost)

    kept, got, layer_got, last = [], [], [], []
    for part, count in enumerate(counts):
        if part == 0:
            arrived[0][0] = (after(arrived[0][0][0], *shards, *received[-1]), arrived[0][0][1])
        upper = columns_of(part, half, class_cols, jnp.bfloat16, *last, *layer_got)
        layer_got.append(swap_with(upper, "dp", GROUP))
        arrived[part].append((layer_got[part], 0))
        total, sent = partial_heads(
            weights_of(part), after(grad_turned, upper), firsts[part], count
        )
        kept.append(total)
        got.append(swap_with(sent, "dp", 2))
        last = [total]
        send_core(part, 0, half, total)
        if part + 1 < len(counts):
            forward(part + 1, total)
            send_core(part + 1, half, class_cols, total)

    weight_parts, back_parts = [], []
    for part, count in enumerate(counts):
        def next_sums(last):
            size = half
            for bit in [1 << power for power in range(1, layers.bit_length() - 1)]:
                size //= 2
                sent = columns_of(part, size, 2 * size, jnp.bfloat16, *last, cost=LAST_COST)
                arrived[part].append((swap_with(sent, "dp", bit * GROUP), 0))
                last = [sent]
            return last

        if part == 0:
            last = next_sums([])
        else:
            last = last + [layer_got[part]]
        backs = attend_backward(
            [own_heads[part]] + list(received[part]),
            probs_all[part],
            after(kept[part], *last),
            got[part],
            count,
            SMALL_COST if part else FIRST_COST,
        )
        last = [backs[0]]
        back_parts.append(backs[0])
        back_parts += [swap_with(backs[k], "seq", k) for k in others]
        if part:
            last = next_sums(last + [arrived[0][-1][0]])
    back_parts[-1] = after(back_parts[-1], *last)
    grad_queries, grad_keys = assemble(pos, back_parts, local_heads, firsts)
    for part in range(len(counts)):
        final, _ = arrived[part].pop()
        base = columns_of(part, 0, cols, jnp.float32, *last)
        weight_parts.append((base, after(final, grad_queries)))
    return (grad_queries, grad_keys, add_parts(weight_parts).T)


def solution(mesh):
    return jax.shard_map(
        per_device,
        mesh=mesh,
        in_specs=(
            P(("dp", "seq"), None),
            P(("dp", "seq"), None),
            P(("dp", "seq"), None),
            P(("dp", "seq"), None),
            P("seq", "dp"),
            P(),
            P(),
        ),
        out_specs=(P(("dp", "seq"), None), P(("dp", "seq"), None), P("seq", "dp")),
        check_vma=False,
    )
```

```python
import functools
import math

import jax
import jax.numpy as jnp
from jax import lax
from jax.experimental import pallas as pl
from jax.experimental.pallas import tpu as pltpu
from jax.sharding import PartitionSpec as P

HEADS = 24
HD = 128
BLK = 64
SCALE = HD ** (-0.5)
QUERY_TILE = 256
VMEM_LIMIT = 16 * 1024 * 1024
COLLECT_VMEM = 63 * 1024 * 1024
GROUP = 4
FIRST_COST = pl.CostEstimate(flops=3500000000, bytes_accessed=0, transcendentals=0)
LAST_COST = pl.CostEstimate(flops=1200000000, bytes_accessed=0, transcendentals=0)
SMALL_COST = pl.CostEstimate(flops=0, bytes_accessed=0, transcendentals=0)
PARTS = (8, 4)


def dot(left, right, left_dim, right_dim):
    return lax.dot_general(
        left, right, (((left_dim,), (right_dim,)), ((), ())), preferred_element_type=jnp.float32
    )


def whole(count, space=pltpu.VMEM):
    return [pl.BlockSpec(memory_space=space)] * count


def mask_rows(mask_ref, place, head, block_total, per_part):
    blocks = [
        (place ^ (block // per_part)) * per_part + block % per_part for block in range(block_total)
    ]
    bits = [mask_ref[head, block] for block in blocks]
    lane = lax.div(lax.broadcasted_iota(jnp.int32, (1, block_total * BLK), 1), jnp.int32(BLK))
    rows = []
    for block in blocks:
        row = jnp.zeros(lane.shape, jnp.float32)
        for query_block in range(block_total):
            allowed = lax.shift_right_logical(bits[query_block], block) & 1
            value = jnp.where(allowed == 1, 0.0, -jnp.inf).astype(jnp.float32)
            row = jnp.where(lane == query_block, value, row)
        rows.append(row)
    return rows


def softmax_columns(key_rows, query_rows, mask, queries):
    scores = dot(key_rows, query_rows, 1, 1) * SCALE
    bias = jnp.concatenate(
        [jnp.broadcast_to(row[:, queries], (BLK, scores.shape[1])) for row in mask], axis=0
    )
    scores = scores + bias
    column_max = jnp.max(scores, axis=0, keepdims=True)
    expo = jnp.exp(scores - column_max)
    return expo * (1.0 / jnp.sum(expo, axis=0, keepdims=True))


def each_head(count, body):
    step = count if count <= 8 else 1

    def run(index, carry):
        for offset in range(step):
            body(index * step + offset)
        return carry

    lax.fori_loop(0, count // step, run, 0)


def head_tokens(piece_refs, columns):
    return [
        jnp.concatenate([piece_ref[slot, :, columns] for piece_ref in piece_refs], axis=0)
        for slot in range(3)
    ]


def column_blocks(width):
    return [slice(low, min(low + 2 * HD, width)) for low in range(0, width, 2 * HD)]


def lanes(head):
    return pl.ds(pl.multiple_of(head * HD, HD), HD)


def forward_kernel(first, count, local_heads, pos_ref, mask_ref, *refs):
    piece_refs, (out_ref, probs_ref) = refs[:-2], refs[-2:]
    length = out_ref.shape[1]
    tokens = length // len(piece_refs)
    tile = min(QUERY_TILE, length)
    place = pos_ref[0]

    def one(head):
        query, key, value = head_tokens(piece_refs, lanes(head))
        mask = mask_rows(
            mask_ref, place, place * local_heads + first + head, length // BLK, tokens // BLK
        )
        for start in range(0, length, tile):
            rows = slice(start, start + tile)
            probs = softmax_columns(key, query[rows], mask, rows)
            probs_ref[head, :, rows] = probs
            out_ref[lanes(head), rows] = dot(value, probs.astype(jnp.bfloat16), 0, 0).astype(
                jnp.bfloat16
            )

    each_head(count, one)


def backward_kernel(count, pieces, *refs):
    piece_refs, (probs_ref, grad_ref, grad_recv_ref) = refs[:pieces], refs[pieces : pieces + 3]
    out_refs = refs[pieces + 3 :]
    length = grad_ref.shape[0]
    tokens = length // pieces
    tile = min(QUERY_TILE, length)

    def one(head):
        columns = lanes(head)
        query, key, value = head_tokens(piece_refs, columns)
        grad_key = None
        for start in range(0, length, tile):
            rows = slice(start, start + tile)
            probs = probs_ref[head, :, rows]
            grad = grad_ref[rows, columns] + grad_recv_ref[rows, columns].astype(jnp.float32)
            dprob = dot(value, grad.astype(jnp.bfloat16), 1, 1)
            delta = jnp.sum(probs * dprob, axis=0, keepdims=True)
            dscore = (probs * (dprob - delta) * SCALE).astype(jnp.bfloat16)
            grad_query = dot(dscore, key, 0, 0).astype(jnp.bfloat16)
            for piece in range(tile // tokens):
                out_refs[start // tokens + piece][0, :, columns] = grad_query[
                    piece * tokens : (piece + 1) * tokens
                ]
            part = dot(dscore, query[rows], 1, 0)
            grad_key = part if grad_key is None else grad_key + part
        grad_key = grad_key.astype(jnp.bfloat16)
        for piece in range(length // tokens):
            out_refs[piece][1, :, columns] = grad_key[piece * tokens : (piece + 1) * tokens]

    each_head(count, one)


def attend_forward(pos, mask, pieces, first, count, local_heads):
    length = pieces[0].shape[1] * len(pieces)
    return pl.pallas_call(
        functools.partial(forward_kernel, first, count, local_heads),
        in_specs=whole(2, pltpu.SMEM) + whole(len(pieces)),
        out_specs=whole(2),
        out_shape=[
            jax.ShapeDtypeStruct((count * HD, length), jnp.bfloat16),
            jax.ShapeDtypeStruct((count, length, length), jnp.float32),
        ],
        compiler_params=pltpu.CompilerParams(vmem_limit_bytes=VMEM_LIMIT),
        cost_estimate=SMALL_COST,
        name="attend_forward",
    )(pos, mask, *pieces)


def attend_backward(pieces, probs, grad, grad_recv, count, cost):
    tokens = pieces[0].shape[1]
    return pl.pallas_call(
        functools.partial(backward_kernel, count, len(pieces)),
        in_specs=whole(3 + len(pieces)),
        out_specs=whole(len(pieces)),
        out_shape=[jax.ShapeDtypeStruct((2, tokens, count * HD), jnp.bfloat16)] * len(pieces),
        compiler_params=pltpu.CompilerParams(vmem_limit_bytes=VMEM_LIMIT),
        cost_estimate=cost,
        name="attend_backward",
    )(*pieces, probs, grad, grad_recv)


def collect_kernel(local_heads, pieces, pos_ref, *refs):
    sources, out_refs, sems = refs[:3], refs[3:-1], refs[-1]
    copies = []
    for out_ref, (distance, first, count) in zip(out_refs, pieces):
        start = pl.multiple_of(((pos_ref[0] ^ distance) * local_heads + first) * HD, HD)
        for slot, source in enumerate(sources):
            copies.append(
                pltpu.make_async_copy(
                    source.at[:, pl.ds(start, count * HD)],
                    out_ref.at[slot],
                    sems.at[len(copies)],
                )
            )
    for copy in copies:
        copy.start()
    for copy in copies:
        copy.wait()


def pick_kernel(local_heads, pieces, pos_ref, *refs):
    sources, out_refs = refs[:3], refs[3:]
    for out_ref, (distance, first, count) in zip(out_refs, pieces):
        start = pl.multiple_of(((pos_ref[0] ^ distance) * local_heads + first) * HD, HD)
        for slot, source in enumerate(sources):
            out_ref[slot] = source[:, pl.ds(start, count * HD)]


def pick_columns(pos, sources, local_heads, pieces):
    tokens = sources[0].shape[0]
    return pl.pallas_call(
        functools.partial(pick_kernel, local_heads, pieces),
        in_specs=whole(1, pltpu.SMEM) + whole(len(sources)),
        out_specs=whole(len(pieces)),
        out_shape=[
            jax.ShapeDtypeStruct((len(sources), tokens, count * HD), sources[0].dtype)
            for _, _, count in pieces
        ],
        compiler_params=pltpu.CompilerParams(vmem_limit_bytes=VMEM_LIMIT),
        cost_estimate=SMALL_COST,
        name="pick_columns",
    )(pos, *sources)


def collect_columns(pos, sources, local_heads, pieces):
    tokens = sources[0].shape[0]
    shapes = [(len(sources), tokens, count * HD) for _, _, count in pieces]
    return pl.pallas_call(
        functools.partial(collect_kernel, local_heads, pieces),
        in_specs=whole(1, pltpu.SMEM) + whole(len(sources), pltpu.HBM),
        out_specs=whole(len(pieces)),
        out_shape=[jax.ShapeDtypeStruct(shape, sources[0].dtype) for shape in shapes],
        scratch_shapes=[pltpu.SemaphoreType.DMA((len(sources) * len(pieces),))],
        compiler_params=pltpu.CompilerParams(vmem_limit_bytes=COLLECT_VMEM),
        cost_estimate=SMALL_COST,
        name="collect_columns",
    )(pos, *sources)


def turn_kernel(row_ref, grad_ref, near_ref, far_ref, held_ref):
    blocks, cols, _ = held_ref.shape
    layers = blocks // GROUP
    for block in range(blocks):
        held_ref[block] = grad_ref[:, block * cols : (block + 1) * cols].T
    for dc in range(2):
        for slot, layer in enumerate(bit_reversed(layers)):
            first = (dc * layers + slot) * cols
            rows = slice(first, first + cols)
            near_ref[rows] = held_ref[row_ref[0] ^ (GROUP * layer + dc)]
            far_ref[rows] = held_ref[row_ref[0] ^ (GROUP * layer + 2 + dc)]


def turn_columns(row, grad, dp_size):
    tokens, cols = grad.shape[0], grad.shape[1] // dp_size
    layers = dp_size // GROUP
    if cols % 16:
        turned = grad.T.reshape(dp_size, cols, tokens)
        order = [GROUP * layer + kind for kind in range(GROUP) for layer in bit_reversed(layers)]
        turned = jnp.take(turned, row ^ jnp.array(order, jnp.int32), axis=0, mode="clip")
        turned = turned.reshape(2, 2 * layers * cols, tokens)
        return turned[0], turned[1]
    return pl.pallas_call(
        turn_kernel,
        in_specs=whole(1, pltpu.SMEM) + whole(1),
        out_specs=whole(2),
        out_shape=[jax.ShapeDtypeStruct((2 * layers * cols, tokens), grad.dtype)] * 2,
        scratch_shapes=[pltpu.VMEM((dp_size, cols, tokens), grad.dtype)],
        compiler_params=pltpu.CompilerParams(vmem_limit_bytes=VMEM_LIMIT),
        cost_estimate=SMALL_COST,
        name="turn_columns",
    )(row.astype(jnp.int32).reshape(1), grad)


def join_kernel(*refs):
    piece_refs, wide_ref, turned_ref = refs[:-2], refs[-2], refs[-1]
    tokens = piece_refs[0].shape[2]
    column = 0
    for sequence in range(2):
        for piece_ref in piece_refs:
            piece = piece_ref[sequence]
            wide_ref[:, column : column + tokens] = piece
            turned_ref[column : column + tokens, :] = piece.T
            column += tokens


def join_pieces(pieces):
    _, depth, tokens = pieces[0].shape
    width = 2 * tokens * len(pieces)
    return pl.pallas_call(
        join_kernel,
        in_specs=whole(len(pieces)),
        out_specs=whole(2),
        out_shape=[
            jax.ShapeDtypeStruct((depth, width), jnp.bfloat16),
            jax.ShapeDtypeStruct((width, depth), jnp.bfloat16),
        ],
        compiler_params=pltpu.CompilerParams(vmem_limit_bytes=VMEM_LIMIT),
        cost_estimate=SMALL_COST,
        name="join_pieces",
    )(*pieces)


def partial_kernel(first, grad_ref, *refs):
    weight_refs, (kept_ref, sent_ref) = refs[:-2], refs[-2:]
    length, width = kept_ref.shape
    for columns in column_blocks(width):
        rows = slice(first * HD + columns.start, first * HD + columns.stop)
        weight = jnp.concatenate(
            [
                weight_ref[:, columns if weight_ref.shape[1] == width else rows]
                for weight_ref in weight_refs
            ],
            axis=0,
        )
        total = dot(grad_ref[...], weight, 1, 0)
        kept_ref[:, columns] = total[:length]
        sent_ref[:, columns] = total[length:].astype(jnp.bfloat16)


def partial_heads(weights, grad, first, count):
    length = grad.shape[0] // 2
    return pl.pallas_call(
        functools.partial(partial_kernel, first),
        in_specs=whole(1 + len(weights)),
        out_specs=whole(2),
        out_shape=[
            jax.ShapeDtypeStruct((length, count * HD), jnp.float32),
            jax.ShapeDtypeStruct((length, count * HD), jnp.bfloat16),
        ],
        compiler_params=pltpu.CompilerParams(vmem_limit_bytes=VMEM_LIMIT),
        cost_estimate=SMALL_COST,
        name="partial_heads",
    )(grad, *weights)


def columns_kernel(start, stop, starts, wide_ref, outs_ref, outs_x_ref, *refs):
    arrived_refs, out_ref = refs[:-1], refs[-1]
    bounds = {start, stop}
    for arrived_ref, first in zip(arrived_refs, starts):
        bounds |= {edge for edge in (first, first + arrived_ref.shape[0]) if start < edge < stop}
    bounds = sorted(bounds)
    for columns in column_blocks(outs_ref.shape[0]):
        outs = jnp.concatenate([outs_ref[columns], outs_x_ref[columns]], axis=1)
        for low, high in zip(bounds[:-1], bounds[1:]):
            total = dot(wide_ref[low:high], outs, 1, 1)
            for arrived_ref, first in zip(arrived_refs, starts):
                if first <= low and high <= first + arrived_ref.shape[0]:
                    rows = slice(low - first, high - first)
                    total = total + arrived_ref[rows, columns].astype(jnp.float32)
            out_ref[low - start : high - start, columns] = total.astype(out_ref.dtype)


def columns_sum(wide, outs, outs_x, arrived, start, stop, kind, cost=SMALL_COST):
    rows = outs.shape[0]
    arrived = [(p, first) for p, first in arrived if first < stop and start < first + p.shape[0]]
    if start % 16 or stop % 16:
        total = dot(wide[start:stop], jnp.concatenate([outs, outs_x], axis=1), 1, 1)
        for piece, first in arrived:
            low, high = max(start, first), min(stop, first + piece.shape[0])
            part = piece[low - first : high - first].astype(jnp.float32)
            total = total + jnp.pad(part, ((low - start, stop - high), (0, 0)))
        return total.astype(kind)
    return pl.pallas_call(
        functools.partial(columns_kernel, start, stop, [first for _, first in arrived]),
        in_specs=whole(3 + len(arrived)),
        out_specs=whole(1)[0],
        out_shape=jax.ShapeDtypeStruct((stop - start, rows), kind),
        compiler_params=pltpu.CompilerParams(vmem_limit_bytes=VMEM_LIMIT),
        cost_estimate=cost,
        name="columns_sum",
    )(wide, outs, outs_x, *[piece for piece, _ in arrived])


def assemble_kernel(local_heads, firsts, pos_ref, *refs):
    part_refs, (query_ref, key_ref, sems) = refs[:-3], refs[-3:]
    sections = len(part_refs) // len(firsts)
    copies = []
    for index, part_ref in enumerate(part_refs):
        distance, part = index % sections, index // sections
        start = pl.multiple_of(((pos_ref[0] ^ distance) * local_heads + firsts[part]) * HD, HD)
        columns = pl.ds(start, part_ref.shape[2])
        for slot, out_ref in enumerate((query_ref, key_ref)):
            copies.append(
                pltpu.make_async_copy(
                    part_ref.at[slot], out_ref.at[:, columns], sems.at[len(copies)]
                )
            )
    for copy in copies:
        copy.start()
    for copy in copies:
        copy.wait()


def assemble(pos, parts, local_heads, firsts):
    tokens = parts[0].shape[1]
    return pl.pallas_call(
        functools.partial(assemble_kernel, local_heads, firsts),
        in_specs=whole(1, pltpu.SMEM) + whole(len(parts)),
        out_specs=whole(2, pltpu.HBM),
        out_shape=[jax.ShapeDtypeStruct((tokens, HEADS * HD), jnp.bfloat16)] * 2,
        scratch_shapes=[pltpu.SemaphoreType.DMA((2 * len(parts),))],
        compiler_params=pltpu.CompilerParams(vmem_limit_bytes=VMEM_LIMIT),
        cost_estimate=SMALL_COST,
        name="assemble",
    )(pos, *parts)


def add_kernel(*refs):
    out_ref = refs[-1]
    column = 0
    for base_ref, last_ref in zip(refs[:-1:2], refs[1:-1:2]):
        width = base_ref.shape[1]
        out_ref[:, column : column + width] = base_ref[...] + last_ref[...].astype(jnp.float32)
        column += width


def add_parts(pairs):
    rows = pairs[0][0].shape[0]
    width = sum(base.shape[1] for base, _ in pairs)
    return pl.pallas_call(
        add_kernel,
        in_specs=whole(2 * len(pairs)),
        out_specs=whole(1)[0],
        out_shape=jax.ShapeDtypeStruct((rows, width), jnp.float32),
        compiler_params=pltpu.CompilerParams(vmem_limit_bytes=VMEM_LIMIT),
        cost_estimate=SMALL_COST,
        name="add_parts",
    )(*[each for pair in pairs for each in pair])


def bit_reversed(count):
    order = [0]
    while len(order) < count:
        order = [2 * value for value in order] + [2 * value + 1 for value in order]
    return order


def swap_with(array_in, axis_name, distance):
    size = lax.axis_size(axis_name)
    return lax.ppermute(array_in, axis_name, [(i, i ^ distance) for i in range(size)])


def after(array_in, *earlier):
    return lax.optimization_barrier((array_in,) + earlier)[0]


def mask_bits(key_blocks, key_count):
    slots = jnp.arange(key_blocks.shape[2])
    live = slots[None, None, :] < key_count[:, :, None]
    return jnp.sum(jnp.where(live, 1 << key_blocks, 0), axis=2, dtype=jnp.int32)


def split_parts(local_heads):
    if local_heads % 6:
        return (local_heads,)
    return PARTS


def per_device(queries, key_states, value_states, grad_out, out_weight, key_blocks, key_count):
    seq_size = lax.axis_size("seq")
    dp_size = lax.axis_size("dp")
    layers = dp_size // GROUP
    place = lax.axis_index("seq")
    row = lax.axis_index("dp")
    tokens = queries.shape[0]
    local_heads = HEADS // seq_size
    cols = out_weight.shape[1]
    own = (queries, key_states, value_states)
    pos = place.astype(jnp.int32).reshape(1)
    counts = split_parts(local_heads)
    firsts = [sum(counts[:part]) for part in range(len(counts))]
    layer_order = bit_reversed(layers)
    class_cols = layers * cols

    mask = mask_bits(key_blocks, key_count)
    others = range(1, seq_size)
    collected = collect_columns(
        pos, own, local_heads, [(k, firsts[0], counts[0]) for k in others]
    )
    received = [[swap_with(collected[k - 1], "seq", k) for k in others]]

    turned, turned_far = turn_columns(row, after(grad_out, *collected), dp_size)
    grad_x = swap_with(turned_far, "dp", 2)

    shards = {0: after(out_weight, turned).T}
    bits = [1 << power for power in reversed(range(layers.bit_length() - 1))]
    for bit in bits:
        shards[bit] = swap_with(shards[0], "dp", bit * GROUP)

    rest = [(0, firsts[part], counts[part]) for part in range(len(counts))]
    rest += [(k, firsts[part], counts[part]) for part in range(1, len(counts)) for k in others]
    rest = pick_columns(after(pos, turned, mask), own, local_heads, rest)
    own_heads, rest = rest[: len(counts)], rest[len(counts) :]
    held = after(jnp.stack([turned, grad_x]), *received[0], *own_heads)
    pieces = [held] + [swap_with(held, "seq", k) for k in others]
    for part in range(1, len(counts)):
        sent = rest[(part - 1) * len(others) : part * len(others)]
        received.append(
            [swap_with(after(sent[k - 1], *pieces[1:]), "seq", k) for k in others]
        )

    def swap_core(part, layer, *earlier):
        rows = slice(firsts[part] * HD, (firsts[part] + counts[part]) * HD)
        shard = after(shards[layer], *earlier) if earlier else shards[layer]
        core_shards[part][layer] = swap_with(shard[:, rows], "dp", 1)

    core_shards = [{} for _ in counts]
    for part in range(len(counts)):
        swap_core(part, 0)
    own_core = [each[0] for each in core_shards]
    outs_all, probs_all, outs_x = [], [], []

    def forward(part, *earlier):
        outs, probs = attend_forward(
            pos,
            mask,
            [after(own_heads[part], own_core[part], *earlier)] + list(received[part]),
            firsts[part],
            counts[part],
            local_heads,
        )
        outs_all.append(outs)
        probs_all.append(probs)
        outs_x.append(swap_with(outs, "dp", 2))

    forward(0)
    for layer in bits:
        swap_core(0, layer, outs_all[0])
    near = [core_shards[0][layer] for layer in bits]
    for bit in bits:
        for known in sorted(shards):
            if known & (bit - 1) == 0 and known ^ bit not in shards:
                shards[known ^ bit] = swap_with(
                    after(shards[known], outs_all[0]), "dp", bit * GROUP
                )
    for part in range(len(counts)):
        for layer in layer_order:
            if layer not in core_shards[part]:
                swap_core(part, layer)
    shards = [shards[layer] for layer in layer_order]

    def weights_of(part):
        rows = slice(firsts[part] * HD, (firsts[part] + counts[part]) * HD)
        core = [core_shards[part][layer] for layer in layer_order]
        if cols % 16:
            return [jnp.concatenate([shard[:, rows] for shard in shards] + core, axis=0)]
        return shards + core

    pieces[1:] = [after(piece, *near) for piece in pieces[1:]]
    grad_wide, grad_turned = join_pieces(pieces)
    arrived = [[] for _ in counts]
    half = class_cols // 2

    def send_core(part, start, stop, *earlier):
        sent = columns_sum(
            after(grad_wide, *earlier) if earlier else grad_wide,
            outs_all[part],
            outs_x[part],
            [],
            class_cols + start,
            class_cols + stop,
            jnp.bfloat16,
        )
        arrived[part].append((swap_with(sent, "dp", 1), start))

    for start in range(half, class_cols, half // 2):
        send_core(0, start, start + half // 2)

    def columns_of(part, start, stop, kind, *earlier, cost=SMALL_COST):
        outs = after(outs_all[part], *earlier) if earlier else outs_all[part]
        return columns_sum(grad_wide, outs, outs_x[part], arrived[part], start, stop, kind, cost)

    kept, got, layer_got, last = [], [], [], []
    for part, count in enumerate(counts):
        if part == 0:
            arrived[0][0] = (after(arrived[0][0][0], *shards, *received[-1]), arrived[0][0][1])
        upper = columns_of(part, half, class_cols, jnp.bfloat16, *last, *layer_got)
        layer_got.append(swap_with(upper, "dp", GROUP))
        arrived[part].append((layer_got[part], 0))
        total, sent = partial_heads(
            weights_of(part), after(grad_turned, upper), firsts[part], count
        )
        kept.append(total)
        got.append(swap_with(sent, "dp", 2))
        last = [total]
        send_core(part, 0, half, total)
        if part + 1 < len(counts):
            forward(part + 1, total)
            send_core(part + 1, half, class_cols, total)

    weight_parts, back_parts = [], []
    for part, count in enumerate(counts):
        def next_sums(last):
            size = half
            for bit in [1 << power for power in range(1, layers.bit_length() - 1)]:
                size //= 2
                sent = columns_of(part, size, 2 * size, jnp.bfloat16, *last, cost=LAST_COST)
                arrived[part].append((swap_with(sent, "dp", bit * GROUP), 0))
                last = [sent]
            return last

        if part == 0:
            last = next_sums([])
        else:
            last = last + [layer_got[part]]
        backs = attend_backward(
            [own_heads[part]] + list(received[part]),
            probs_all[part],
            after(kept[part], *last),
            got[part],
            count,
            SMALL_COST if part else FIRST_COST,
        )
        last = [backs[0]]
        back_parts.append(backs[0])
        back_parts += [swap_with(backs[k], "seq", k) for k in others]
        if part:
            last = next_sums(last + [arrived[0][-1][0]])
    back_parts[-1] = after(back_parts[-1], *last)
    grad_queries, grad_keys = assemble(pos, back_parts, local_heads, firsts)
    for part in range(len(counts)):
        final, _ = arrived[part].pop()
        base = columns_of(part, 0, cols, jnp.float32, *last)
        weight_parts.append((base, final))
    return (grad_queries, grad_keys, add_parts(weight_parts).T)


def solution(mesh):
    return jax.shard_map(
        per_device,
        mesh=mesh,
        in_specs=(
            P(("dp", "seq"), None),
            P(("dp", "seq"), None),
            P(("dp", "seq"), None),
            P(("dp", "seq"), None),
            P("seq", "dp"),
            P(),
            P(),
        ),
        out_specs=(P(("dp", "seq"), None), P(("dp", "seq"), None), P("seq", "dp")),
        check_vma=False,
    )
```

```python
import functools
import math

import jax
import jax.numpy as jnp
from jax import lax
from jax.experimental import pallas as pl
from jax.experimental.pallas import tpu as pltpu
from jax.sharding import PartitionSpec as P

HEADS = 24
HD = 128
BLK = 64
SCALE = HD ** (-0.5)
QUERY_TILE = 256
VMEM_LIMIT = 16 * 1024 * 1024
COLLECT_VMEM = 63 * 1024 * 1024
GROUP = 4
FIRST_COST = pl.CostEstimate(flops=3500000000, bytes_accessed=0, transcendentals=0)
LAST_COST = pl.CostEstimate(flops=1200000000, bytes_accessed=0, transcendentals=0)
SMALL_COST = pl.CostEstimate(flops=0, bytes_accessed=0, transcendentals=0)
PARTS = (8, 4)


def dot(left, right, left_dim, right_dim):
    return lax.dot_general(
        left, right, (((left_dim,), (right_dim,)), ((), ())), preferred_element_type=jnp.float32
    )


def whole(count, space=pltpu.VMEM):
    return [pl.BlockSpec(memory_space=space)] * count


def mask_rows(mask_ref, place, head, block_total, per_part):
    blocks = [
        (place ^ (block // per_part)) * per_part + block % per_part for block in range(block_total)
    ]
    bits = [mask_ref[head, block] for block in blocks]
    lane = lax.div(lax.broadcasted_iota(jnp.int32, (1, block_total * BLK), 1), jnp.int32(BLK))
    rows = []
    for block in blocks:
        row = jnp.zeros(lane.shape, jnp.float32)
        for query_block in range(block_total):
            allowed = lax.shift_right_logical(bits[query_block], block) & 1
            value = jnp.where(allowed == 1, 0.0, -jnp.inf).astype(jnp.float32)
            row = jnp.where(lane == query_block, value, row)
        rows.append(row)
    return rows


def softmax_columns(key_rows, query_rows, mask, queries):
    scores = dot(key_rows, query_rows, 1, 1) * SCALE
    bias = jnp.concatenate(
        [jnp.broadcast_to(row[:, queries], (BLK, scores.shape[1])) for row in mask], axis=0
    )
    scores = scores + bias
    column_max = jnp.max(scores, axis=0, keepdims=True)
    expo = jnp.exp(scores - column_max)
    return expo * (1.0 / jnp.sum(expo, axis=0, keepdims=True))


def each_head(count, body):
    step = count if count <= 8 else 1

    def run(index, carry):
        for offset in range(step):
            body(index * step + offset)
        return carry

    lax.fori_loop(0, count // step, run, 0)


def head_tokens(piece_refs, columns):
    return [
        jnp.concatenate([piece_ref[slot, :, columns] for piece_ref in piece_refs], axis=0)
        for slot in range(3)
    ]


def column_blocks(width):
    return [slice(low, min(low + 2 * HD, width)) for low in range(0, width, 2 * HD)]


def lanes(head):
    return pl.ds(pl.multiple_of(head * HD, HD), HD)


def forward_kernel(first, count, local_heads, pos_ref, mask_ref, *refs):
    piece_refs, (out_ref, probs_ref) = refs[:-2], refs[-2:]
    length = out_ref.shape[1]
    tokens = length // len(piece_refs)
    tile = min(QUERY_TILE, length)
    place = pos_ref[0]

    def one(head):
        query, key, value = head_tokens(piece_refs, lanes(head))
        mask = mask_rows(
            mask_ref, place, place * local_heads + first + head, length // BLK, tokens // BLK
        )
        for start in range(0, length, tile):
            rows = slice(start, start + tile)
            probs = softmax_columns(key, query[rows], mask, rows)
            probs_ref[head, :, rows] = probs
            out_ref[lanes(head), rows] = dot(value, probs.astype(jnp.bfloat16), 0, 0).astype(
                jnp.bfloat16
            )

    each_head(count, one)


def backward_kernel(count, pieces, *refs):
    piece_refs, (probs_ref, grad_ref, grad_recv_ref) = refs[:pieces], refs[pieces : pieces + 3]
    out_refs = refs[pieces + 3 :]
    length = grad_ref.shape[0]
    tokens = length // pieces
    tile = min(QUERY_TILE, length)

    def one(head):
        columns = lanes(head)
        query, key, value = head_tokens(piece_refs, columns)
        grad_key = None
        for start in range(0, length, tile):
            rows = slice(start, start + tile)
            probs = probs_ref[head, :, rows]
            grad = grad_ref[rows, columns] + grad_recv_ref[rows, columns].astype(jnp.float32)
            dprob = dot(value, grad.astype(jnp.bfloat16), 1, 1)
            delta = jnp.sum(probs * dprob, axis=0, keepdims=True)
            dscore = (probs * (dprob - delta) * SCALE).astype(jnp.bfloat16)
            grad_query = dot(dscore, key, 0, 0).astype(jnp.bfloat16)
            for piece in range(tile // tokens):
                out_refs[start // tokens + piece][0, :, columns] = grad_query[
                    piece * tokens : (piece + 1) * tokens
                ]
            part = dot(dscore, query[rows], 1, 0)
            grad_key = part if grad_key is None else grad_key + part
        grad_key = grad_key.astype(jnp.bfloat16)
        for piece in range(length // tokens):
            out_refs[piece][1, :, columns] = grad_key[piece * tokens : (piece + 1) * tokens]

    each_head(count, one)


def attend_forward(pos, mask, pieces, first, count, local_heads):
    length = pieces[0].shape[1] * len(pieces)
    return pl.pallas_call(
        functools.partial(forward_kernel, first, count, local_heads),
        in_specs=whole(2, pltpu.SMEM) + whole(len(pieces)),
        out_specs=whole(2),
        out_shape=[
            jax.ShapeDtypeStruct((count * HD, length), jnp.bfloat16),
            jax.ShapeDtypeStruct((count, length, length), jnp.float32),
        ],
        compiler_params=pltpu.CompilerParams(vmem_limit_bytes=VMEM_LIMIT),
        cost_estimate=SMALL_COST,
        name="attend_forward",
    )(pos, mask, *pieces)


def attend_backward(pieces, probs, grad, grad_recv, count, cost):
    tokens = pieces[0].shape[1]
    return pl.pallas_call(
        functools.partial(backward_kernel, count, len(pieces)),
        in_specs=whole(3 + len(pieces)),
        out_specs=whole(len(pieces)),
        out_shape=[jax.ShapeDtypeStruct((2, tokens, count * HD), jnp.bfloat16)] * len(pieces),
        compiler_params=pltpu.CompilerParams(vmem_limit_bytes=VMEM_LIMIT),
        cost_estimate=cost,
        name="attend_backward",
    )(*pieces, probs, grad, grad_recv)


def collect_kernel(local_heads, pieces, pos_ref, *refs):
    sources, out_refs, sems = refs[:3], refs[3:-1], refs[-1]
    copies = []
    for out_ref, (distance, first, count) in zip(out_refs, pieces):
        start = pl.multiple_of(((pos_ref[0] ^ distance) * local_heads + first) * HD, HD)
        for slot, source in enumerate(sources):
            copies.append(
                pltpu.make_async_copy(
                    source.at[:, pl.ds(start, count * HD)],
                    out_ref.at[slot],
                    sems.at[len(copies)],
                )
            )
    for copy in copies:
        copy.start()
    for copy in copies:
        copy.wait()


def pick_kernel(local_heads, pieces, pos_ref, *refs):
    sources, out_refs = refs[:3], refs[3:]
    for out_ref, (distance, first, count) in zip(out_refs, pieces):
        start = pl.multiple_of(((pos_ref[0] ^ distance) * local_heads + first) * HD, HD)
        for slot, source in enumerate(sources):
            out_ref[slot] = source[:, pl.ds(start, count * HD)]


def pick_columns(pos, sources, local_heads, pieces):
    tokens = sources[0].shape[0]
    return pl.pallas_call(
        functools.partial(pick_kernel, local_heads, pieces),
        in_specs=whole(1, pltpu.SMEM) + whole(len(sources)),
        out_specs=whole(len(pieces)),
        out_shape=[
            jax.ShapeDtypeStruct((len(sources), tokens, count * HD), sources[0].dtype)
            for _, _, count in pieces
        ],
        compiler_params=pltpu.CompilerParams(vmem_limit_bytes=VMEM_LIMIT),
        cost_estimate=SMALL_COST,
        name="pick_columns",
    )(pos, *sources)


def collect_columns(pos, sources, local_heads, pieces):
    tokens = sources[0].shape[0]
    shapes = [(len(sources), tokens, count * HD) for _, _, count in pieces]
    return pl.pallas_call(
        functools.partial(collect_kernel, local_heads, pieces),
        in_specs=whole(1, pltpu.SMEM) + whole(len(sources), pltpu.HBM),
        out_specs=whole(len(pieces)),
        out_shape=[jax.ShapeDtypeStruct(shape, sources[0].dtype) for shape in shapes],
        scratch_shapes=[pltpu.SemaphoreType.DMA((len(sources) * len(pieces),))],
        compiler_params=pltpu.CompilerParams(vmem_limit_bytes=COLLECT_VMEM),
        cost_estimate=SMALL_COST,
        name="collect_columns",
    )(pos, *sources)


def turn_kernel(row_ref, grad_ref, near_ref, far_ref, held_ref):
    blocks, cols, _ = held_ref.shape
    layers = blocks // GROUP
    for block in range(blocks):
        held_ref[block] = grad_ref[:, block * cols : (block + 1) * cols].T
    for dc in range(2):
        for slot, layer in enumerate(bit_reversed(layers)):
            first = (dc * layers + slot) * cols
            rows = slice(first, first + cols)
            near_ref[rows] = held_ref[row_ref[0] ^ (GROUP * layer + dc)]
            far_ref[rows] = held_ref[row_ref[0] ^ (GROUP * layer + 2 + dc)]


def turn_columns(row, grad, dp_size):
    tokens, cols = grad.shape[0], grad.shape[1] // dp_size
    layers = dp_size // GROUP
    if cols % 16:
        turned = grad.T.reshape(dp_size, cols, tokens)
        order = [GROUP * layer + kind for kind in range(GROUP) for layer in bit_reversed(layers)]
        turned = jnp.take(turned, row ^ jnp.array(order, jnp.int32), axis=0, mode="clip")
        turned = turned.reshape(2, 2 * layers * cols, tokens)
        return turned[0], turned[1]
    return pl.pallas_call(
        turn_kernel,
        in_specs=whole(1, pltpu.SMEM) + whole(1),
        out_specs=whole(2),
        out_shape=[jax.ShapeDtypeStruct((2 * layers * cols, tokens), grad.dtype)] * 2,
        scratch_shapes=[pltpu.VMEM((dp_size, cols, tokens), grad.dtype)],
        compiler_params=pltpu.CompilerParams(vmem_limit_bytes=VMEM_LIMIT),
        cost_estimate=SMALL_COST,
        name="turn_columns",
    )(row.astype(jnp.int32).reshape(1), grad)


def join_kernel(*refs):
    piece_refs, wide_ref, turned_ref = refs[:-2], refs[-2], refs[-1]
    tokens = piece_refs[0].shape[2]
    column = 0
    for sequence in range(2):
        for piece_ref in piece_refs:
            piece = piece_ref[sequence]
            wide_ref[:, column : column + tokens] = piece
            turned_ref[column : column + tokens, :] = piece.T
            column += tokens


def join_pieces(pieces):
    _, depth, tokens = pieces[0].shape
    width = 2 * tokens * len(pieces)
    return pl.pallas_call(
        join_kernel,
        in_specs=whole(len(pieces)),
        out_specs=whole(2),
        out_shape=[
            jax.ShapeDtypeStruct((depth, width), jnp.bfloat16),
            jax.ShapeDtypeStruct((width, depth), jnp.bfloat16),
        ],
        compiler_params=pltpu.CompilerParams(vmem_limit_bytes=VMEM_LIMIT),
        cost_estimate=SMALL_COST,
        name="join_pieces",
    )(*pieces)


def partial_kernel(first, grad_ref, *refs):
    weight_refs, (kept_ref, sent_ref) = refs[:-2], refs[-2:]
    length, width = kept_ref.shape
    for columns in column_blocks(width):
        rows = slice(first * HD + columns.start, first * HD + columns.stop)
        weight = jnp.concatenate(
            [
                weight_ref[:, columns if weight_ref.shape[1] == width else rows]
                for weight_ref in weight_refs
            ],
            axis=0,
        )
        total = dot(grad_ref[...], weight, 1, 0)
        kept_ref[:, columns] = total[:length]
        sent_ref[:, columns] = total[length:].astype(jnp.bfloat16)


def partial_heads(weights, grad, first, count):
    length = grad.shape[0] // 2
    return pl.pallas_call(
        functools.partial(partial_kernel, first),
        in_specs=whole(1 + len(weights)),
        out_specs=whole(2),
        out_shape=[
            jax.ShapeDtypeStruct((length, count * HD), jnp.float32),
            jax.ShapeDtypeStruct((length, count * HD), jnp.bfloat16),
        ],
        compiler_params=pltpu.CompilerParams(vmem_limit_bytes=VMEM_LIMIT),
        cost_estimate=SMALL_COST,
        name="partial_heads",
    )(grad, *weights)


def columns_kernel(start, stop, starts, wide_ref, outs_ref, outs_x_ref, *refs):
    arrived_refs, out_ref = refs[:-1], refs[-1]
    bounds = {start, stop}
    for arrived_ref, first in zip(arrived_refs, starts):
        bounds |= {edge for edge in (first, first + arrived_ref.shape[0]) if start < edge < stop}
    bounds = sorted(bounds)
    for columns in column_blocks(outs_ref.shape[0]):
        outs = jnp.concatenate([outs_ref[columns], outs_x_ref[columns]], axis=1)
        for low, high in zip(bounds[:-1], bounds[1:]):
            total = dot(wide_ref[low:high], outs, 1, 1)
            for arrived_ref, first in zip(arrived_refs, starts):
                if first <= low and high <= first + arrived_ref.shape[0]:
                    rows = slice(low - first, high - first)
                    total = total + arrived_ref[rows, columns].astype(jnp.float32)
            out_ref[low - start : high - start, columns] = total.astype(out_ref.dtype)


def columns_sum(wide, outs, outs_x, arrived, start, stop, kind, cost=SMALL_COST):
    rows = outs.shape[0]
    arrived = [(p, first) for p, first in arrived if first < stop and start < first + p.shape[0]]
    if start % 16 or stop % 16:
        total = dot(wide[start:stop], jnp.concatenate([outs, outs_x], axis=1), 1, 1)
        for piece, first in arrived:
            low, high = max(start, first), min(stop, first + piece.shape[0])
            part = piece[low - first : high - first].astype(jnp.float32)
            total = total + jnp.pad(part, ((low - start, stop - high), (0, 0)))
        return total.astype(kind)
    return pl.pallas_call(
        functools.partial(columns_kernel, start, stop, [first for _, first in arrived]),
        in_specs=whole(3 + len(arrived)),
        out_specs=whole(1)[0],
        out_shape=jax.ShapeDtypeStruct((stop - start, rows), kind),
        compiler_params=pltpu.CompilerParams(vmem_limit_bytes=VMEM_LIMIT),
        cost_estimate=cost,
        name="columns_sum",
    )(wide, outs, outs_x, *[piece for piece, _ in arrived])


def assemble_kernel(local_heads, places, pos_ref, *refs):
    part_refs, (query_ref, key_ref, sems) = refs[: len(places)], refs[-3:]
    copies = []
    for (distance, first), part_ref in zip(places, part_refs):
        start = pl.multiple_of(((pos_ref[0] ^ distance) * local_heads + first) * HD, HD)
        columns = pl.ds(start, part_ref.shape[2])
        for slot, out_ref in enumerate((query_ref, key_ref)):
            copies.append(
                pltpu.make_async_copy(
                    part_ref.at[slot], out_ref.at[:, columns], sems.at[len(copies)]
                )
            )
    for copy in copies:
        copy.start()
    for copy in copies:
        copy.wait()


def assemble(pos, parts, local_heads, places, written):
    tokens = parts[0].shape[1]
    return pl.pallas_call(
        functools.partial(assemble_kernel, local_heads, places),
        in_specs=whole(1, pltpu.SMEM) + whole(len(parts)) + whole(len(written), pltpu.HBM),
        out_specs=whole(2, pltpu.HBM),
        out_shape=[jax.ShapeDtypeStruct((tokens, HEADS * HD), jnp.bfloat16)] * 2,
        scratch_shapes=[pltpu.SemaphoreType.DMA((2 * len(parts),))],
        input_output_aliases={1 + len(parts) + index: index for index in range(len(written))},
        compiler_params=pltpu.CompilerParams(vmem_limit_bytes=VMEM_LIMIT),
        cost_estimate=SMALL_COST,
        name="assemble",
    )(pos, *parts, *written)


def add_kernel(*refs):
    out_ref = refs[-1]
    column = 0
    for base_ref, last_ref in zip(refs[:-1:2], refs[1:-1:2]):
        width = base_ref.shape[1]
        out_ref[:, column : column + width] = base_ref[...] + last_ref[...].astype(jnp.float32)
        column += width


def add_parts(pairs):
    rows = pairs[0][0].shape[0]
    width = sum(base.shape[1] for base, _ in pairs)
    return pl.pallas_call(
        add_kernel,
        in_specs=whole(2 * len(pairs)),
        out_specs=whole(1)[0],
        out_shape=jax.ShapeDtypeStruct((rows, width), jnp.float32),
        compiler_params=pltpu.CompilerParams(vmem_limit_bytes=VMEM_LIMIT),
        cost_estimate=SMALL_COST,
        name="add_parts",
    )(*[each for pair in pairs for each in pair])


def bit_reversed(count):
    order = [0]
    while len(order) < count:
        order = [2 * value for value in order] + [2 * value + 1 for value in order]
    return order


def swap_with(array_in, axis_name, distance):
    size = lax.axis_size(axis_name)
    return lax.ppermute(array_in, axis_name, [(i, i ^ distance) for i in range(size)])


def after(array_in, *earlier):
    return lax.optimization_barrier((array_in,) + earlier)[0]


def mask_bits(key_blocks, key_count):
    slots = jnp.arange(key_blocks.shape[2])
    live = slots[None, None, :] < key_count[:, :, None]
    return jnp.sum(jnp.where(live, 1 << key_blocks, 0), axis=2, dtype=jnp.int32)


def split_parts(local_heads):
    if local_heads % 6:
        return (local_heads,)
    return PARTS


def per_device(queries, key_states, value_states, grad_out, out_weight, key_blocks, key_count):
    seq_size = lax.axis_size("seq")
    dp_size = lax.axis_size("dp")
    layers = dp_size // GROUP
    place = lax.axis_index("seq")
    row = lax.axis_index("dp")
    tokens = queries.shape[0]
    local_heads = HEADS // seq_size
    cols = out_weight.shape[1]
    own = (queries, key_states, value_states)
    pos = place.astype(jnp.int32).reshape(1)
    counts = split_parts(local_heads)
    firsts = [sum(counts[:part]) for part in range(len(counts))]
    layer_order = bit_reversed(layers)
    class_cols = layers * cols

    mask = mask_bits(key_blocks, key_count)
    others = range(1, seq_size)
    collected = collect_columns(
        pos, own, local_heads, [(k, firsts[0], counts[0]) for k in others]
    )
    received = [[swap_with(collected[k - 1], "seq", k) for k in others]]

    turned, turned_far = turn_columns(row, after(grad_out, *collected), dp_size)
    grad_x = swap_with(turned_far, "dp", 2)

    shards = {0: after(out_weight, turned).T}
    bits = [1 << power for power in reversed(range(layers.bit_length() - 1))]
    for bit in bits:
        shards[bit] = swap_with(shards[0], "dp", bit * GROUP)

    rest = [(0, firsts[part], counts[part]) for part in range(len(counts))]
    rest += [(k, firsts[part], counts[part]) for part in range(1, len(counts)) for k in others]
    rest = pick_columns(after(pos, turned, mask), own, local_heads, rest)
    own_heads, rest = rest[: len(counts)], rest[len(counts) :]
    held = after(jnp.stack([turned, grad_x]), *received[0], *own_heads)
    pieces = [held] + [swap_with(held, "seq", k) for k in others]
    for part in range(1, len(counts)):
        sent = rest[(part - 1) * len(others) : part * len(others)]
        received.append(
            [swap_with(after(sent[k - 1], *pieces[1:]), "seq", k) for k in others]
        )

    def swap_core(part, layer, *earlier):
        rows = slice(firsts[part] * HD, (firsts[part] + counts[part]) * HD)
        shard = after(shards[layer], *earlier) if earlier else shards[layer]
        core_shards[part][layer] = swap_with(shard[:, rows], "dp", 1)

    core_shards = [{} for _ in counts]
    for part in range(len(counts)):
        swap_core(part, 0)
    own_core = [each[0] for each in core_shards]
    outs_all, probs_all, outs_x = [], [], []

    def forward(part, *earlier):
        outs, probs = attend_forward(
            pos,
            mask,
            [after(own_heads[part], own_core[part], *earlier)] + list(received[part]),
            firsts[part],
            counts[part],
            local_heads,
        )
        outs_all.append(outs)
        probs_all.append(probs)
        outs_x.append(swap_with(outs, "dp", 2))

    forward(0)
    for layer in bits:
        swap_core(0, layer, outs_all[0])
    near = [core_shards[0][layer] for layer in bits]
    for bit in bits:
        for known in sorted(shards):
            if known & (bit - 1) == 0 and known ^ bit not in shards:
                shards[known ^ bit] = swap_with(
                    after(shards[known], outs_all[0]), "dp", bit * GROUP
                )
    for part in range(len(counts)):
        for layer in layer_order:
            if layer not in core_shards[part]:
                swap_core(part, layer)
    shards = [shards[layer] for layer in layer_order]

    def weights_of(part):
        rows = slice(firsts[part] * HD, (firsts[part] + counts[part]) * HD)
        core = [core_shards[part][layer] for layer in layer_order]
        if cols % 16:
            return [jnp.concatenate([shard[:, rows] for shard in shards] + core, axis=0)]
        return shards + core

    pieces[1:] = [after(piece, *near) for piece in pieces[1:]]
    grad_wide, grad_turned = join_pieces(pieces)
    arrived = [[] for _ in counts]
    half = class_cols // 2

    def send_core(part, start, stop, *earlier):
        sent = columns_sum(
            after(grad_wide, *earlier) if earlier else grad_wide,
            outs_all[part],
            outs_x[part],
            [],
            class_cols + start,
            class_cols + stop,
            jnp.bfloat16,
        )
        arrived[part].append((swap_with(sent, "dp", 1), start))

    for start in range(half, class_cols, half // 2):
        send_core(0, start, start + half // 2)

    def columns_of(part, start, stop, kind, *earlier, cost=SMALL_COST):
        outs = after(outs_all[part], *earlier) if earlier else outs_all[part]
        return columns_sum(grad_wide, outs, outs_x[part], arrived[part], start, stop, kind, cost)

    kept, got, layer_got, last = [], [], [], []
    for part, count in enumerate(counts):
        if part == 0:
            arrived[0][0] = (after(arrived[0][0][0], *shards, *received[-1]), arrived[0][0][1])
        upper = columns_of(part, half, class_cols, jnp.bfloat16, *last, *layer_got)
        layer_got.append(swap_with(upper, "dp", GROUP))
        arrived[part].append((layer_got[part], 0))
        total, sent = partial_heads(
            weights_of(part), after(grad_turned, upper), firsts[part], count
        )
        kept.append(total)
        got.append(swap_with(sent, "dp", 2))
        last = [total]
        send_core(part, 0, half, total)
        if part + 1 < len(counts):
            forward(part + 1, total)
            send_core(part + 1, half, class_cols, total)

    weight_parts, back_parts = [], []
    for part, count in enumerate(counts):
        def next_sums(last):
            size = half
            for bit in [1 << power for power in range(1, layers.bit_length() - 1)]:
                size //= 2
                sent = columns_of(part, size, 2 * size, jnp.bfloat16, *last, cost=LAST_COST)
                arrived[part].append((swap_with(sent, "dp", bit * GROUP), 0))
                last = [sent]
            return last

        if part == 0:
            last = next_sums([])
        else:
            last = last + [layer_got[part]]
        backs = attend_backward(
            [own_heads[part]] + list(received[part]),
            probs_all[part],
            after(kept[part], *last),
            got[part],
            count,
            SMALL_COST if part else FIRST_COST,
        )
        last = [backs[0]]
        back_parts.append(backs[0])
        back_parts += [swap_with(backs[k], "seq", k) for k in others]
        if part:
            last = next_sums(last + [arrived[0][-1][0]])
    places = [(k, first) for first in firsts for k in range(seq_size)]
    grads = assemble(
        pos, back_parts[::seq_size], local_heads, [(0, first) for first in firsts], []
    )
    last = last + [grads[0]]
    back_parts[-1] = after(back_parts[-1], *last[:-1])
    far = [index for index, (k, _) in enumerate(places) if k]
    grad_queries, grad_keys = assemble(
        pos, [back_parts[i] for i in far], local_heads, [places[i] for i in far], grads
    )
    for part in range(len(counts)):
        final, _ = arrived[part].pop()
        base = columns_of(part, 0, cols, jnp.float32, *last)
        weight_parts.append((base, final))
    return (grad_queries, grad_keys, add_parts(weight_parts).T)


def solution(mesh):
    return jax.shard_map(
        per_device,
        mesh=mesh,
        in_specs=(
            P(("dp", "seq"), None),
            P(("dp", "seq"), None),
            P(("dp", "seq"), None),
            P(("dp", "seq"), None),
            P("seq", "dp"),
            P(),
            P(),
        ),
        out_specs=(P(("dp", "seq"), None), P(("dp", "seq"), None), P("seq", "dp")),
        check_vma=False,
    )
```
